128 devices in a mesh: region: 8 (over z, core), block: 16 (over y, x).
Axes of the slice: x: 4, y: 4, z: 4, core: 2. Of those that a mesh axis runs over, the one named last changes fastest.
Arguments:
- point_feats: bfloat16 [393216, 64], P(('region', 'block')), may hold values from -6 to 6
- point_block: int32 [393216, 1], P(('region', 'block')), may hold values from 0 to 15; in each aligned block of 3072 rows (0 to 3071, 3072 to 6143, ...) at most 384 rows name the same one
- point_voxel: int32 [393216], P(('region', 'block')), may hold values from 0 to 4095
- neighbours: int32 [128, 6], P(('region', 'block')), may hold values from -1 to 127, as said below
- conv_one: bfloat16 [27, 64, 64], replicated, may hold values from -0.15625 to 0.15625
- bias_one: float32 [64], replicated, may hold values from -3 to 3
- conv_two: bfloat16 [27, 64, 64], replicated, may hold values from -0.15625 to 0.15625
- bias_two: float32 [64], replicated, may hold values from -3 to 3
Outputs:
- encoded: bfloat16 [128, 16, 16, 16, 64], P(('region', 'block'))
The draws below stay inside these ranges and needn't reach their ends.
Inputs may be any that keep to these rules, and one draw needn't show every extreme that they name: `point_block`: within the rows of one device no block is named by more than 384 points, and some block is named by exactly 384. `neighbours`: links are symmetric: if face f of block g names block h, face f xor 1 of h names g. Faces 2 to 5 name only blocks of the same device. Faces 0 and 1 name a block of the same device or one of the device with the same block index and region index one lower (face 0) or one higher (face 1); on each device exactly one block has face 1 naming a block on the next region (none on the last region), and exactly one has face 0 naming a block on the previous region (none on the first).
All inputs are finite; a program needn't handle non-finite values.
Results may differ from the reference program's by a relative error of at most 0.0045.
Values may be sent and summed in bfloat16 or wider, within the bound.
A program may use at most 128 MiB of HBM per device.

```python
import math
import jax
import jax.numpy as jnp
import numpy as np
from jax import lax

C = 64
BE = 16
BLK_DEV = 1
PTS_DEV = 3072
VOX = 4096
REGIONS = 8
COLUMNS = 16
BLOCKS_REG = 16
POINTS = 393216
CAP = 384


def draw_neighbours(key, part):
    key = jax.random.fold_in(key, 7)
    devices_all = REGIONS * COLUMNS
    key_order, key_yperm, key_ylive, key_zperm, key_zlive = jax.random.split(key, 5)

    def permute_rows(subkey):
        return jax.vmap(lambda inner: jax.random.permutation(inner, BLK_DEV))(jax.random.split(subkey, devices_all)).astype(jnp.int32)
    device = jnp.arange(devices_all, dtype=jnp.int32)[:, None] * jnp.ones((1, BLK_DEV), jnp.int32)
    slots = jnp.arange(BLK_DEV, dtype=jnp.int32)[None, :] + 0 * device
    region_of = device // COLUMNS
    order = permute_rows(key_order)
    place = jnp.argsort(order, axis=1).astype(jnp.int32)
    next_dev = jnp.minimum(device + COLUMNS, devices_all - 1)
    prev_dev = jnp.maximum(device - COLUMNS, 0)
    later = jnp.minimum(place + 1, BLK_DEV - 1)
    earlier = jnp.maximum(place - 1, 0)
    same_next = device * BLK_DEV + jnp.take_along_axis(order, later, axis=1)
    same_prev = device * BLK_DEV + jnp.take_along_axis(order, earlier, axis=1)
    cross_next = next_dev * BLK_DEV + order[next_dev, 0]
    cross_prev = prev_dev * BLK_DEV + order[prev_dev, BLK_DEV - 1]
    plus_x = jnp.where(place + 1 < BLK_DEV, same_next, jnp.where(region_of + 1 < REGIONS, cross_next, -1))
    minus_x = jnp.where(place > 0, same_prev, jnp.where(region_of > 0, cross_prev, -1))

    def links(key_perm, key_live):
        permuted = permute_rows(key_perm)
        inverse = jnp.argsort(permuted, axis=1).astype(jnp.int32)
        alive = (jax.random.randint(key_live, (devices_all, BLK_DEV), 0, 10) < 7) & (permuted != slots)
        plus_side = jnp.where(alive, device * BLK_DEV + permuted, -1)
        back_alive = jnp.take_along_axis(alive, inverse, axis=1)
        minus_side = jnp.where(back_alive, device * BLK_DEV + inverse, -1)
        return (minus_side, plus_side)
    minus_y, plus_y = links(key_yperm, key_ylive)
    minus_z, plus_z = links(key_zperm, key_zlive)
    stacked = jnp.stack([minus_x, plus_x, minus_y, plus_y, minus_z, plus_z], axis=-1)
    return stacked.reshape(devices_all * BLK_DEV, 6).astype(jnp.int32)


def touch_ends(array, rng, low, top_value):
    longest = array.shape.index(max(array.shape))
    spots = []
    for shift in (0, 1):
        where = [jax.random.randint(jax.random.fold_in(rng, axis), (), 0, length) for axis, length in enumerate(array.shape)]
        where[longest] = (where[longest] + shift) % array.shape[longest]
        spots.append(tuple(where))
    return array.at[spots[0]].set(low).at[spots[1]].set(top_value)


def level_of(rng, shape, shards, low, high):
    def one(position, parts):
        draws = jax.random.uniform(jax.random.fold_in(jax.random.fold_in(rng, 6), position), (parts,), jnp.float32, low / len(shards), high / len(shards))
        return jnp.repeat(jnp.exp(draws), shape[position] // parts).reshape((-1,) + (1,) * (len(shape) - position - 1))

    loudness = one(*shards[0])
    for cut in shards[1:]:
        loudness = loudness * one(*cut)
    return loudness


def deal_out(own_key, own, number, rows, count, top, reach, slope):
    ranking = jax.random.permutation(own_key, count)
    packed, usual = load_shares(count, rows * top, reach, slope, True), load_shares(count, rows * top, reach, slope, False)
    places = jnp.arange(count)

    def named(sizes, turn):
        used = int((sizes > 0).sum())
        fixed = max(1, used // 4)
        passed = fixed + (places - fixed + turn * (used - fixed)) % max(1, count - fixed)
        return jnp.zeros((count,), jnp.int32).at[ranking[jnp.where(places < fixed, places, passed)]].set(jnp.asarray(sizes, jnp.int32))

    sizes = jnp.where(number % 4 == 0, named(packed, number // 4), named(usual, number - number // 4 - 1))
    mixed = jax.random.permutation(jax.random.fold_in(own, 3), count)
    giver, taker = mixed[0:count // 2 * 2:2], mixed[1:count // 2 * 2:2]
    slack = jnp.minimum(sizes[giver] - 1, reach - sizes[taker]) // 2
    slack = jnp.where((giver == ranking[0]) | (taker == ranking[0]) | (sizes[taker] == 0), 0, jnp.maximum(slack, 0))
    passed = jax.random.randint(jax.random.fold_in(own, 4), (count // 2,), 0, 1 << 20) % (slack + 1)
    sizes = sizes.at[giver].add(-passed).at[taker].add(passed)
    labels = jnp.searchsorted(jnp.cumsum(sizes), jnp.arange(rows * top), side="right").astype(jnp.int32)
    grid = labels.reshape(top, rows).T
    grid = grid[jax.random.permutation(jax.random.fold_in(own, 1), rows)]
    turn = jax.random.randint(jax.random.fold_in(own, 2), (rows, 1), 0, top)
    return jnp.take_along_axis(grid, (jnp.arange(top)[None, :] + turn) % top, axis=1)


def load_shares(number_of, total, bound, slope, full):
    portions = [(1 << 20) // math.isqrt(rank ** slope) + 1 for rank in range(1, number_of + 1)]
    largest = bound if full else min(bound, max(-(-total // number_of), total * portions[0] // sum(portions)))
    least = 1 if total - largest >= number_of - 1 else 0
    given, rest = [largest] + [least] * (number_of - 1), total - largest - least * (number_of - 1)
    while rest > 0:
        movable = [i for i in range(1, number_of) if given[i] < largest] or [i for i in range(1, number_of) if given[i] < bound]
        mass, remaining = sum([portions[i] for i in movable]), rest
        for i in movable:
            extra = min(bound - given[i], max(1, remaining * portions[i] // mass), rest)
            given[i] = given[i] + extra
            rest = rest - extra
    return np.array(given)


def scatter_about(own_key, dims, width, reach, cuts=(), kind=jnp.bfloat16):
    values = width * jax.random.normal(own_key, dims, jnp.float32)
    if cuts:
        values = values * level_of(own_key, dims, cuts, -0.22, 0.18)
    return jnp.clip(values, -reach, reach).astype(kind)


def setup_inputs(seed: int = 0) -> dict:
    key_of = jax.random.split(jax.random.key(seed), 9)
    point_feats = scatter_about(key_of[0], (POINTS, C), 1.0, 6.0, ((0, 128),))
    point_block_keys = jax.random.split(jax.random.fold_in(key_of[1], 1), POINTS // PTS_DEV)
    point_block_turns = jax.random.permutation(jax.random.fold_in(key_of[1], 3), POINTS // PTS_DEV)
    point_block = jax.vmap(lambda own, number: deal_out(jax.random.fold_in(key_of[1], 2), own, number, PTS_DEV, BLOCKS_REG, 1, CAP, 1))(point_block_keys, point_block_turns).reshape((POINTS, 1))
    point_voxel = touch_ends(jax.random.randint(key_of[2], (POINTS,), 0, VOX), jax.random.fold_in(key_of[2], 1), 0, VOX - 1).astype(jnp.int32)
    neighbours = draw_neighbours(jax.random.fold_in(key_of[8], 71), 0)
    conv_one = scatter_about(key_of[4], (27, C, C), (27 * C) ** -0.5, 0.15625)
    bias_one = scatter_about(key_of[5], (C,), 0.5, 3.0, (), jnp.float32)
    conv_two = scatter_about(key_of[6], (27, C, C), (27 * C) ** -0.5, 0.15625)
    bias_two = scatter_about(key_of[7], (C,), 0.5, 3.0, (), jnp.float32)
    return {"point_feats": point_feats, "point_block": point_block, "point_voxel": point_voxel, "neighbours": neighbours, "conv_one": conv_one, "bias_one": bias_one, "conv_two": conv_two, "bias_two": bias_two}


def layer_sides(single):
    return [single[0], single[-1], single[:, 0], single[:, -1], single[:, :, 0], single[:, :, -1]]


def padded_block(single, layers):
    padded = jnp.pad(single, ((1, 1), (1, 1), (1, 1), (0, 0)))
    padded = padded.at[0, 1:-1, 1:-1].set(layers[0])
    padded = padded.at[-1, 1:-1, 1:-1].set(layers[1])
    padded = padded.at[1:-1, 0, 1:-1].set(layers[2])
    padded = padded.at[1:-1, -1, 1:-1].set(layers[3])
    padded = padded.at[1:-1, 1:-1, 0].set(layers[4])
    padded = padded.at[1:-1, 1:-1, -1].set(layers[5])
    return padded


def convolve(padded, weight):
    pieces = []
    for step_x in range(3):
        for step_y in range(3):
            for step_z in range(3):
                patch = padded[step_x:step_x + BE, step_y:step_y + BE, step_z:step_z + BE]
                pieces.append(patch.reshape(VOX, C).astype(jnp.float32))
    stacked = jnp.concatenate(pieces, axis=1)
    return jnp.dot(stacked, weight.reshape(27 * C, C).astype(jnp.float32), preferred_element_type=jnp.float32)


def encode_layer(blocks, neighbours, weight, bias_vec, occupied, residual_in):
    def single_block(block_id):
        single = blocks[block_id]
        layers = []
        for face in range(6):
            source_id = neighbours[block_id, face]
            source = blocks[jnp.maximum(source_id, 0)]
            keeping = (source_id >= 0).astype(single.dtype)
            layers.append(layer_sides(source)[face ^ 1] * keeping)
        total = convolve(padded_block(single, layers), weight) + bias_vec
        if residual_in is not None:
            total = total + residual_in[block_id].reshape(VOX, C).astype(jnp.float32)
        result = jnp.maximum(total, 0.0) * occupied[block_id].reshape(VOX, 1)
        return result.astype(jnp.bfloat16).reshape(BE, BE, BE, C)

    return lax.map(single_block, jnp.arange(blocks.shape[0], dtype=jnp.int32))


def reference(point_feats, point_block, point_voxel, neighbours, conv_one, bias_one, conv_two, bias_two):
    blocks_region = BLK_DEV * COLUMNS
    block_total = blocks_region * REGIONS
    row_ids = jnp.arange(point_feats.shape[0], dtype=jnp.int32)
    region_ids = row_ids // (PTS_DEV * COLUMNS)
    owner = region_ids * blocks_region + point_block[:, 0]
    segment = owner * VOX + point_voxel
    voxel_sum = jax.ops.segment_sum(point_feats.astype(jnp.float32), segment, num_segments=block_total * VOX)
    counted = jax.ops.segment_sum(jnp.ones(segment.shape, jnp.float32), segment, num_segments=block_total * VOX)
    voxels = (voxel_sum / jnp.maximum(counted, 1.0)[:, None]).astype(jnp.bfloat16)
    voxels = voxels.reshape(block_total, BE, BE, BE, C)
    occupied = (counted > 0.5).astype(jnp.float32).reshape(block_total, VOX)
    hidden = encode_layer(voxels, neighbours, conv_one, bias_one, occupied, None)
    return encode_layer(hidden, neighbours, conv_two, bias_two, occupied, voxels)
```

```python
import functools
import math

import jax
import jax.numpy as jnp
from jax import lax
from jax.experimental import pallas as pl
from jax.experimental.pallas import tpu as pltpu
from jax.sharding import PartitionSpec as P

BE = 16
C = 64
ROWS = BE * BE
ZG = 4
WIDE = 4 * C
ZPAD = (BE + 2) * C
TAP = 6 * C
NT = (((1,), (1,)), ((), ()))
F32 = jnp.float32
BF16 = jnp.bfloat16
MESH = pl.DeviceIdType.MESH


def iota(shape, dim):
    return lax.broadcasted_iota(jnp.int32, shape, dim)


def onehot(ids, row):
    return jnp.where(ids == row, jnp.ones((), BF16), jnp.zeros((), BF16))


def ranks_of(blk, columns):
    points = blk.shape[1]
    chunks = points // 256
    member = (iota((columns, points), 0) == blk).astype(F32)
    stacked = jnp.concatenate(
        [member[:, k * 256 : (k + 1) * 256] for k in range(chunks)], axis=0
    ).astype(BF16)
    before = (iota((256, 256), 0) < iota((256, 256), 1)).astype(F32).astype(BF16)
    prefix = jnp.dot(stacked, before, preferred_element_type=F32)
    totals = jnp.dot(stacked, jnp.ones((256, 256), BF16), preferred_element_type=F32)
    running = jnp.zeros((columns, 256), F32)
    rows = []
    for k in range(chunks):
        part = slice(k * columns, (k + 1) * columns)
        own = member[:, k * 256 : (k + 1) * 256]
        rows.append(jnp.sum(own * (prefix[part] + running), axis=0, keepdims=True))
        running = running + totals[part]
    return jnp.concatenate(rows, axis=1)


def build_weights(conv_ref, wide_ref):
    wide_ref[...] = jnp.zeros_like(wide_ref)

    def one(t, carry):
        w0, w1, w2 = conv_ref[3 * t], conv_ref[3 * t + 1], conv_ref[3 * t + 2]
        none = jnp.zeros_like(w0)
        pairs = ((w0, none), (w1, w0), (w2, w1), (none, w2))
        for k, pair in enumerate(pairs):
            tile = jnp.concatenate(pair, axis=1)
            for half in range(2):
                start = pl.multiple_of(t * TAP + (k + 2 * half) * C, C)
                wide_ref[pl.ds(start, C), half * 128 : (half + 1) * 128] = tile
        return carry

    lax.fori_loop(0, 9, one, 0)


def place_plane(field_ref, plane, groups, keep_y, keep_z):
    lane = iota((BE, 128), 1)
    rolled = []
    for group in groups:
        for half in range(2):
            rolled.append(pltpu.roll(group[:, half * 128 : (half + 1) * 128], 64, 1))
    before = [rolled[-1] * keep_z] + rolled
    after = rolled + [rolled[0] * keep_z]
    wide = jnp.concatenate(
        [jnp.where(lane < C, b, a) for b, a in zip(before, after)], axis=1
    )
    row, col = iota((BE, ZPAD), 0), iota((BE, ZPAD), 1)
    inner = ((col >= C) & (col < ZPAD - C)).astype(F32) * keep_y
    down = pltpu.roll(wide, 1, 0)
    down = jnp.where(row == 0, down * inner, down)
    up = pltpu.roll(wide, BE - 1, 0)
    up = jnp.where(row == BE - 1, up * inner, up)
    rows = pl.ds(pl.multiple_of(plane * BE, BE), BE)
    field_ref[0, rows, :] = down.astype(BF16)
    field_ref[1, rows, :] = wide.astype(BF16)
    field_ref[2, rows, :] = up.astype(BF16)


def convolve(field_ref, wide_ref, plane, count):
    def window(tap, group):
        dx, dy = divmod(tap, 3)
        start = (plane + dx) * BE
        return field_ref[dy, start : start + count * BE, group * WIDE : group * WIDE + TAP]

    total = None
    for first in range(0, 9, 2):
        taps = [t for t in (first, first + 1) if t < 9]
        left = jnp.concatenate(
            [
                jnp.concatenate([window(t, group) for t in taps], axis=1)
                for group in range(ZG)
            ],
            axis=0,
        )
        right = wide_ref[first * TAP : (first + len(taps)) * TAP, :]
        part = jnp.dot(left, right, preferred_element_type=F32)
        total = part if total is None else total + part
    return total


def body(
    dims, feats_ref, blk_ref, vox_ref, link_ref, one_ref, bone_ref, two_ref, btwo_ref, out_ref,
    expanded, indices, send, recv, sums, counts, inverse, voxels, field, wide_one, wide_two,
    side_out, side_in, send_sem, recv_sem, side_send, side_recv,
):
    regions, columns = dims
    side = math.isqrt(columns)
    points = blk_ref.shape[1]
    cap = 2 * points // columns
    quarter = cap // 4
    region, block = lax.axis_index("region"), lax.axis_index("block")
    my_y, my_x = block // side, block % side

    def at(dy, dx):
        return lax.rem(my_y + dy, side) * side + lax.rem(my_x + dx, side)

    barrier = pltpu.get_barrier_semaphore()
    for dy in range(side):
        for dx in range(side):
            if dy or dx:
                pl.semaphore_signal(
                    barrier, inc=1, device_id=(region, at(dy, dx)), device_id_type=MESH
                )

    @pl.when(region > 0)
    def _():
        pl.semaphore_signal(barrier, inc=1, device_id=(region - 1, block), device_id_type=MESH)

    @pl.when(region < regions - 1)
    def _():
        pl.semaphore_signal(barrier, inc=1, device_id=(region + 1, block), device_id_type=MESH)

    blk = blk_ref[...]
    rank = ranks_of(blk, columns)
    low = (
        (rank >= quarter).astype(F32)
        + (rank >= 2 * quarter).astype(F32)
        + (rank >= 3 * quarter).astype(F32)
    )
    high = rank - quarter * low
    feats = feats_ref[...]
    for k in range(4):
        expanded[k * C : (k + 1) * C, :] = feats * (low == k).astype(F32).astype(BF16)

    third = (rank >= 128).astype(F32) + (rank >= 256).astype(F32)
    place = (rank - 128 * third).astype(BF16)
    number = vox_ref[...]
    code_a = (number // 64 + 1).astype(F32).astype(BF16)
    code_b = (number % 64).astype(F32).astype(BF16)
    slot_row = (blk.astype(F32) * 16 + third).astype(BF16)
    where_to = onehot(iota((columns * 16, points), 0).astype(F32).astype(BF16), slot_row)
    spots = onehot(iota((128, points), 0).astype(F32).astype(BF16), place)
    codes = jnp.concatenate([spots * code_a, spots * code_b], axis=0)
    indices[...] = lax.dot_general(where_to, codes, NT, preferred_element_type=F32).astype(BF16)

    arrivals = columns - 1 + (region > 0).astype(jnp.int32) + (region < regions - 1).astype(jnp.int32)
    pl.semaphore_wait(barrier, arrivals)

    def copy_to(slot, target):
        return pltpu.make_async_remote_copy(
            src_ref=send.at[slot],
            dst_ref=recv.at[slot],
            send_sem=send_sem.at[slot],
            recv_sem=recv_sem.at[slot],
            device_id=(region, target),
            device_id_type=MESH,
        )

    def send_group(step, carry):
        turn = lax.rem(step + 1, side)
        targets = [at(j, lax.rem(turn + j, side)) for j in range(side)]
        blocks = blk_ref[...]
        placing = jnp.concatenate(
            [
                onehot(
                    iota((quarter, points), 0).astype(F32).astype(BF16),
                    jnp.where(blocks == target, high, -1.0).astype(BF16),
                )
                for target in targets
            ],
            axis=0,
        )
        packed = lax.dot_general(placing, expanded[...], NT, preferred_element_type=F32)
        packed = packed.astype(BF16)
        for j, target in enumerate(targets):
            slot = turn * side + j
            mine = packed[j * quarter : (j + 1) * quarter]
            codes_here = indices[pl.ds(pl.multiple_of(target * 16, 16), 16), :]

            def ship():
                send[slot, 0:quarter, :] = mine
                send[slot, quarter : quarter + 16, :] = codes_here
                copy_to(slot, target).start()

            if j == 0:

                @pl.when(turn == 0)
                def _():
                    recv[0, 0:quarter, :] = mine
                    recv[0, quarter : quarter + 16, :] = codes_here

                pl.when(turn != 0)(ship)
            else:
                ship()
        return carry

    lax.fori_loop(0, side, send_group, 0)

    build_weights(one_ref, wide_one)
    build_weights(two_ref, wide_two)

    sums[...] = jnp.zeros_like(sums)
    counts[...] = jnp.zeros_like(counts)

    def bin_group(step, carry):
        turn = lax.rem(step + 1, side)
        hots, masked, flat_hots, depth_hots = [], [], [], []
        for j in range(side):
            slot = turn * side + j
            if j == 0:
                pl.when(turn != 0)(lambda: copy_to(slot, block).wait_recv())
            else:
                copy_to(slot, block).wait_recv()
            code = recv[slot, quarter : quarter + 16, :].astype(F32)[0:8]
            a = code[:, 0:128].astype(jnp.int32) - 1
            b = code[:, 128:256].astype(jnp.int32)
            flat = a * 4 + (b >> 4)
            deep = (b >> 2) & 3
            inner = (b & 3).astype(F32)
            level = jnp.where(a >= 0, b & 15, -1).astype(F32)
            flat = flat.astype(F32)
            pieces = cap // 128
            ids = iota((ROWS, 128), 0).astype(F32).astype(BF16)
            by_group = []
            for group in range(ZG):
                row = jnp.where(deep == group, flat, -1.0)
                by_group.append(
                    jnp.concatenate(
                        [onehot(ids, row[k : k + 1].astype(BF16)) for k in range(pieces)], axis=1
                    )
                )
            hots.append(jnp.concatenate(by_group, axis=0))
            flat_hots.append(
                jnp.concatenate(
                    [onehot(ids, flat[k : k + 1].astype(BF16)) for k in range(pieces)], axis=1
                )
            )
            depth_hots.append(
                jnp.concatenate(
                    [onehot(ids[:BE], level[k : k + 1].astype(BF16)) for k in range(pieces)], axis=1
                )
            )
            turned = inner.T
            of_lane = (iota((128, WIDE), 1) // C).astype(F32)
            choose = jnp.concatenate(
                [(turned[:, k : k + 1] == of_lane).astype(F32) for k in range(pieces)], axis=0
            ).astype(BF16)
            quads = []
            for k in range(4):
                piece = recv[slot, 0:quarter, k * C : (k + 1) * C]
                quads.append(jnp.concatenate([piece] * 4, axis=1))
            masked.append(jnp.concatenate(quads, axis=0) * choose)
        hot = jnp.concatenate(hots, axis=1)
        sums[...] += jnp.dot(hot, jnp.concatenate(masked, axis=0), preferred_element_type=F32)
        counts[...] += lax.dot_general(
            jnp.concatenate(flat_hots, axis=1),
            jnp.concatenate(depth_hots, axis=1),
            NT,
            preferred_element_type=F32,
        )
        return carry

    lax.fori_loop(0, side, bin_group, 0)

    tally = counts[...]
    share = jnp.where(tally > 0.5, 1.0 / jnp.maximum(tally, 1.0), 0.0)
    first = share.astype(BF16)
    rest = share - first.astype(F32)
    second = rest.astype(BF16)
    third_part = (rest - second.astype(F32)).astype(BF16)
    spread = jnp.where(iota((BE, BE * C), 0) == iota((BE, BE * C), 1) // C, 1.0, 0.0).astype(BF16)
    inverse[...] = (
        jnp.dot(first, spread, preferred_element_type=F32)
        + jnp.dot(second, spread, preferred_element_type=F32)
        + jnp.dot(third_part, spread, preferred_element_type=F32)
    )

    keep_y = (link_ref[0, 2] >= 0).astype(F32)
    keep_z = (link_ref[0, 4] >= 0).astype(F32)

    def side_copy(layer, up):
        k = 2 * layer + up
        return pltpu.make_async_remote_copy(
            src_ref=side_out.at[k],
            dst_ref=side_in.at[k],
            send_sem=side_send.at[k],
            recv_sem=side_recv.at[k],
            device_id=(region + 1 if up else region - 1, block),
            device_id_type=MESH,
        )

    def send_sides(layer):
        pl.when(region > 0)(lambda: side_copy(layer, 0).start())
        pl.when(region < regions - 1)(lambda: side_copy(layer, 1).start())

    def receive_sides(layer):
        def put(k, plane):
            groups = [side_in[k, :, z * WIDE : (z + 1) * WIDE].astype(F32) for z in range(ZG)]
            place_plane(field.at[layer], plane, groups, 0.0, 0.0)

        def blank(plane):
            field[layer, :, plane * BE : (plane + 1) * BE, :] = jnp.zeros((3, BE, ZPAD), BF16)

        @pl.when(region > 0)
        def _():
            side_copy(layer, 1).wait_recv()
            put(2 * layer + 1, 0)

        @pl.when(region < regions - 1)
        def _():
            side_copy(layer, 0).wait_recv()
            put(2 * layer, BE + 1)

        pl.when(region == 0)(lambda: blank(0))
        pl.when(region == regions - 1)(lambda: blank(BE + 1))

    def settle_sides(layer):
        pl.when(region > 0)(lambda: side_copy(layer, 0).wait_send())
        pl.when(region < regions - 1)(lambda: side_copy(layer, 1).wait_send())

    def mean_plane(x):
        rows = pl.ds(pl.multiple_of(x * BE, BE), BE)
        groups = []
        for z in range(ZG):
            total = sums[pl.ds(pl.multiple_of(z * ROWS + x * BE, BE), BE), :]
            mean = (total * inverse[rows, z * WIDE : (z + 1) * WIDE]).astype(BF16)
            voxels[rows, z * WIDE : (z + 1) * WIDE] = mean
            groups.append(mean.astype(F32))
        place_plane(field.at[0], x + 1, groups, keep_y, keep_z)

    mean_plane(0)
    mean_plane(BE - 1)
    side_out[0] = voxels[0:BE, :]
    side_out[1] = voxels[ROWS - BE : ROWS, :]
    send_sides(0)
    lax.fori_loop(1, BE - 1, lambda x, carry: (mean_plane(x), carry)[1], 0)

    def encode(layer, plane, count, bias, save):
        total = convolve(field.at[layer], wide_one if layer == 0 else wide_two, plane, count)
        for x in range(count):
            rows = slice((plane + x) * BE, (plane + x + 1) * BE)
            groups = []
            for z in range(ZG):
                cols = slice(z * WIDE, (z + 1) * WIDE)
                start = z * count * BE + x * BE
                value = total[start : start + BE] + bias
                if layer:
                    value = value + voxels[rows, cols].astype(F32)
                value = jnp.where(inverse[rows, cols] > 0.0, jnp.maximum(value, 0.0), 0.0)
                groups.append(value)
            save(plane + x, groups)

    bias_one = jnp.concatenate([bone_ref[...]] * 4, axis=1)
    bias_two = jnp.concatenate([btwo_ref[...]] * 4, axis=1)

    def save_hidden(x, groups):
        groups = [g.astype(BF16) for g in groups]
        if x in (0, BE - 1):
            for z in range(ZG):
                side_out[2 if x == 0 else 3, :, z * WIDE : (z + 1) * WIDE] = groups[z]
        place_plane(field.at[1], x + 1, [g.astype(F32) for g in groups], keep_y, keep_z)

    def save_out(x, groups):
        for z in range(ZG):
            out_ref[x * BE : (x + 1) * BE, z * WIDE : (z + 1) * WIDE] = groups[z].astype(BF16)

    encode(0, 1, BE - 2, bias_one, save_hidden)
    receive_sides(0)
    encode(0, 0, 1, bias_one, save_hidden)
    encode(0, BE - 1, 1, bias_one, save_hidden)
    send_sides(1)
    encode(1, 1, BE - 2, bias_two, save_out)
    receive_sides(1)
    encode(1, 0, 1, bias_two, save_out)
    encode(1, BE - 1, 1, bias_two, save_out)

    def settle(slot, carry):
        copy_to(slot, block).wait_send()
        return carry

    lax.fori_loop(1, columns, settle, 0)
    settle_sides(0)
    settle_sides(1)


def per_device(
    dims, point_feats, point_block, point_voxel, neighbours, conv_one, bias_one, conv_two, bias_two
):
    regions, columns = dims
    points = point_feats.shape[0]
    quarter = 2 * points // columns // 4
    vmem = pl.BlockSpec(memory_space=pltpu.VMEM)
    smem = pl.BlockSpec(memory_space=pltpu.SMEM)
    flat = pl.pallas_call(
        functools.partial(body, dims),
        out_shape=jax.ShapeDtypeStruct((ROWS, BE * C), BF16),
        in_specs=[vmem, vmem, vmem, smem, vmem, vmem, vmem, vmem],
        out_specs=vmem,
        scratch_shapes=[
            pltpu.VMEM((WIDE, points), BF16),
            pltpu.VMEM((columns * 16, 256), BF16),
            pltpu.VMEM((columns, quarter + 16, WIDE), BF16),
            pltpu.VMEM((columns, quarter + 16, WIDE), BF16),
            pltpu.VMEM((ZG * ROWS, WIDE), F32),
            pltpu.VMEM((ROWS, BE), F32),
            pltpu.VMEM((ROWS, BE * C), F32),
            pltpu.VMEM((ROWS, BE * C), BF16),
            pltpu.VMEM((2, 3, (BE + 2) * BE, ZPAD), BF16),
            pltpu.VMEM((9 * TAP, WIDE), BF16),
            pltpu.VMEM((9 * TAP, WIDE), BF16),
            pltpu.VMEM((4, BE, BE * C), BF16),
            pltpu.VMEM((4, BE, BE * C), BF16),
            pltpu.SemaphoreType.DMA((columns,)),
            pltpu.SemaphoreType.DMA((columns,)),
            pltpu.SemaphoreType.DMA((4,)),
            pltpu.SemaphoreType.DMA((4,)),
        ],
        compiler_params=pltpu.CompilerParams(
            collective_id=0, has_side_effects=True, vmem_limit_bytes=56 * 2**20
        ),
    )(
        point_feats.T,
        point_block.T,
        point_voxel.reshape(1, points),
        neighbours,
        conv_one,
        bias_one.reshape(1, C),
        conv_two,
        bias_two.reshape(1, C),
    )
    return flat.reshape(1, BE, BE, BE, C)


def solution(mesh):
    dims = (mesh.shape["region"], mesh.shape["block"])
    return jax.shard_map(
        functools.partial(per_device, dims),
        mesh=mesh,
        in_specs=(
            P(("region", "block"), None),
            P(("region", "block"), None),
            P(("region", "block")),
            P(("region", "block"), None),
            P(),
            P(),
            P(),
            P(),
        ),
        out_specs=P(("region", "block"), None, None, None, None),
        check_vma=False,
    )
```

```python
import functools
import math

import jax
import jax.numpy as jnp
from jax import lax
from jax.experimental import pallas as pl
from jax.experimental.pallas import tpu as pltpu
from jax.sharding import PartitionSpec as P

BE = 16
C = 64
ROWS = BE * BE
ZG = 4
BATCH = 4
PARTS = 8
UNROLL = 16
WIDE = 4 * C
ZPAD = (BE + 2) * C
TAP = 6 * C
NT = (((1,), (1,)), ((), ()))
F32 = jnp.float32
BF16 = jnp.bfloat16
MESH = pl.DeviceIdType.MESH


def iota(shape, dim):
    return lax.broadcasted_iota(jnp.int32, shape, dim)


def onehot(ids, row):
    return jnp.where(ids == row, jnp.ones((), BF16), jnp.zeros((), BF16))


def ranks_of(blk, columns):
    points = blk.shape[1]
    chunks = points // 256
    member = (iota((columns, points), 0) == blk).astype(F32)
    stacked = jnp.concatenate(
        [member[:, k * 256 : (k + 1) * 256] for k in range(chunks)], axis=0
    ).astype(BF16)
    before = (iota((256, 256), 0) < iota((256, 256), 1)).astype(F32).astype(BF16)
    prefix = jnp.dot(stacked, before, preferred_element_type=F32)
    totals = jnp.dot(stacked, jnp.ones((256, 256), BF16), preferred_element_type=F32)
    running = jnp.zeros((columns, 256), F32)
    rows = []
    for k in range(chunks):
        part = slice(k * columns, (k + 1) * columns)
        own = member[:, k * 256 : (k + 1) * 256]
        rows.append(jnp.sum(own * (prefix[part] + running), axis=0, keepdims=True))
        running = running + totals[part]
    return jnp.concatenate(rows, axis=1)


def build_weights(conv_ref, wide_ref):
    wide_ref[...] = jnp.zeros_like(wide_ref)

    def one(t, carry):
        w0, w1, w2 = conv_ref[3 * t], conv_ref[3 * t + 1], conv_ref[3 * t + 2]
        none = jnp.zeros_like(w0)
        pairs = ((w0, none), (w1, w0), (w2, w1), (none, w2))
        for k, pair in enumerate(pairs):
            tile = jnp.concatenate(pair, axis=1)
            for half in range(2):
                start = pl.multiple_of(t * TAP + (k + 2 * half) * C, C)
                wide_ref[pl.ds(start, C), half * 128 : (half + 1) * 128] = tile
        return carry

    lax.fori_loop(0, 9, one, 0)


def place_plane(field_ref, plane, groups, keep_y, keep_z):
    lane = iota((BE, 128), 1)
    rolled = []
    for group in groups:
        for half in range(2):
            rolled.append(pltpu.roll(group[:, half * 128 : (half + 1) * 128], 64, 1))
    before = [rolled[-1] * keep_z] + rolled
    after = rolled + [rolled[0] * keep_z]
    wide = jnp.concatenate(
        [jnp.where(lane < C, b, a) for b, a in zip(before, after)], axis=1
    )
    row, col = iota((BE, ZPAD), 0), iota((BE, ZPAD), 1)
    inner = ((col >= C) & (col < ZPAD - C)).astype(F32) * keep_y
    down = pltpu.roll(wide, 1, 0)
    down = jnp.where(row == 0, down * inner, down)
    up = pltpu.roll(wide, BE - 1, 0)
    up = jnp.where(row == BE - 1, up * inner, up)
    rows = pl.ds(pl.multiple_of(plane * BE, BE), BE)
    field_ref[0, rows, :] = down.astype(BF16)
    field_ref[1, rows, :] = wide.astype(BF16)
    field_ref[2, rows, :] = up.astype(BF16)


def convolve(field_ref, wide_ref, runs):
    def window(tap, group):
        dx, dy = divmod(tap, 3)
        cols = slice(group * WIDE, group * WIDE + TAP)
        return [field_ref[dy, (p + dx) * BE : (p + dx + n) * BE, cols] for p, n in runs]

    total = None
    for first in range(0, 9, 2):
        taps = [t for t in (first, first + 1) if t < 9]
        columns = [
            jnp.concatenate([part for group in range(ZG) for part in window(t, group)], axis=0)
            for t in taps
        ]
        right = wide_ref[first * TAP : (first + len(taps)) * TAP, :]
        part = jnp.dot(jnp.concatenate(columns, axis=1), right, preferred_element_type=F32)
        total = part if total is None else total + part
    return total


def body(
    dims, feats_hbm, blk_ref, vox_hbm, link_ref, one_hbm, bone_ref, two_hbm, btwo_ref, out_ref,
    feats_ref, vox_ref, one_ref, two_ref,
    expanded, indices, send, recv, sums, counts, inverse, voxels, hidden, field, wide_one, wide_two,
    side_out, side_in, send_sem, recv_sem, side_send, side_recv, load_sem,
):
    regions, columns = dims
    side = math.isqrt(columns)
    points = blk_ref.shape[1]
    cap = 2 * points // columns
    quarter = cap // 4
    region, block = lax.axis_index("region"), lax.axis_index("block")
    my_y, my_x = block // side, block % side
    loads = [
        pltpu.make_async_copy(source, target, load_sem.at[k])
        for k, (source, target) in enumerate(
            [(vox_hbm, vox_ref), (feats_hbm, feats_ref), (one_hbm, one_ref), (two_hbm, two_ref)]
        )
    ]
    for load in loads:
        load.start()

    def at(dy, dx):
        return lax.rem(my_y + dy, side) * side + lax.rem(my_x + dx, side)

    barrier = pltpu.get_barrier_semaphore()
    for dy in range(side):
        for dx in range(side):
            if dy or dx:
                pl.semaphore_signal(
                    barrier, inc=1, device_id=(region, at(dy, dx)), device_id_type=MESH
                )

    @pl.when(region > 0)
    def _():
        pl.semaphore_signal(barrier, inc=1, device_id=(region - 1, block), device_id_type=MESH)

    @pl.when(region < regions - 1)
    def _():
        pl.semaphore_signal(barrier, inc=1, device_id=(region + 1, block), device_id_type=MESH)

    blk = blk_ref[...]
    rank = ranks_of(blk, columns)
    low = (
        (rank >= quarter).astype(F32)
        + (rank >= 2 * quarter).astype(F32)
        + (rank >= 3 * quarter).astype(F32)
    )
    high = rank - quarter * low
    loads[0].wait()
    loads[1].wait()
    feats = feats_ref[...]
    for k in range(4):
        expanded[k * C : (k + 1) * C, :] = feats * (low == k).astype(F32).astype(BF16)

    third = (rank >= 128).astype(F32) + (rank >= 256).astype(F32)
    place = (rank - 128 * third).astype(BF16)
    number = vox_ref[...]
    code_a = (number // 64 + 1).astype(F32).astype(BF16)
    code_b = (number % 64).astype(F32).astype(BF16)
    slot_row = (blk.astype(F32) * 8 + third).astype(BF16)
    where_to = onehot(iota((columns * 8, points), 0).astype(F32).astype(BF16), slot_row)
    spots = onehot(iota((128, points), 0).astype(F32).astype(BF16), place)
    codes = jnp.concatenate([spots * code_a, spots * code_b], axis=0)
    coded = lax.dot_general(where_to, codes, NT, preferred_element_type=F32)
    for k in range(columns):
        pair = [coded[k * 8 : (k + 1) * 8, half * 128 : (half + 1) * 128] for half in range(2)]
        indices[k * 16 : (k + 1) * 16, :] = jnp.concatenate(pair, axis=0).astype(BF16)

    arrivals = columns - 1 + (region > 0).astype(jnp.int32) + (region < regions - 1).astype(jnp.int32)
    pl.semaphore_wait(barrier, arrivals)

    def copy_to(slot, target):
        return pltpu.make_async_remote_copy(
            src_ref=send.at[slot],
            dst_ref=recv.at[slot],
            send_sem=send_sem.at[slot],
            recv_sem=recv_sem.at[slot],
            device_id=(region, target),
            device_id_type=MESH,
        )

    def send_group(step, carry):
        turn = lax.rem(step + 1, side)
        targets = [at(j, lax.rem(turn + j, side)) for j in range(side)]
        blocks = blk_ref[...]
        placing = jnp.concatenate(
            [
                onehot(
                    iota((quarter, points), 0).astype(F32).astype(BF16),
                    jnp.where(blocks == target, high, -1.0).astype(BF16),
                )
                for target in targets
            ],
            axis=0,
        )
        packed = lax.dot_general(placing, expanded[...], NT, preferred_element_type=F32)
        packed = packed.astype(BF16)
        for j, target in enumerate(targets):
            slot = turn * side + j
            mine = packed[j * quarter : (j + 1) * quarter]
            codes_here = indices[pl.ds(pl.multiple_of(target * 16, 16), 16), :]

            def fill(pack):
                pack[slot, 0:quarter, :] = mine[:, 0:128]
                pack[slot, quarter : 2 * quarter, :] = mine[:, 128:256]
                pack[slot, 2 * quarter : 2 * quarter + 16, :] = codes_here

            def ship():
                fill(send)
                copy_to(slot, target).start()

            if j == 0:

                pl.when(turn == 0)(lambda: fill(recv))
                pl.when(turn != 0)(ship)
            else:
                ship()
        return carry

    lax.fori_loop(0, side, send_group, 0)

    loads[2].wait()
    build_weights(one_ref, wide_one)
    loads[3].wait()
    build_weights(two_ref, wide_two)

    sums[...] = jnp.zeros_like(sums)
    counts[...] = jnp.zeros_like(counts)

    def bin_group(step, carry):
        hots, masked, flat_hots, depth_hots = [], [], [], []
        for j in range(BATCH):
            turn = step * BATCH + j
            slot = jnp.where(turn == 0, 0, lax.rem(turn + side - 2, columns - 1) + 1)
            if j == 0:
                pl.when(turn != 0)(lambda: copy_to(slot, block).wait_recv())
            else:
                copy_to(slot, block).wait_recv()
            code = recv[slot, 2 * quarter : 2 * quarter + 16, :].astype(F32)
            a = code[0:8].astype(jnp.int32) - 1
            b = code[8:16].astype(jnp.int32)
            flat = a * 4 + (b >> 4)
            deep = (b >> 2) & 3
            inner = (b & 3).astype(F32)
            flat = flat.astype(F32)
            pieces = cap // 128
            ids = iota((ROWS, 128), 0).astype(F32).astype(BF16)
            by_group = []
            for group in range(ZG):
                row = jnp.where(deep == group, flat, -1.0)
                by_group.append(
                    jnp.concatenate(
                        [onehot(ids, row[k : k + 1].astype(BF16)) for k in range(pieces)], axis=1
                    )
                )
            hots.append(jnp.concatenate(by_group, axis=0))
            coarse, fine = a.astype(F32), b.astype(F32)
            for hot_list, value in ((flat_hots, coarse), (depth_hots, fine)):
                hot_list.append(
                    jnp.concatenate(
                        [onehot(ids[:64], value[k : k + 1].astype(BF16)) for k in range(pieces)], axis=1
                    )
                )
            turned = inner.T
            of_lane = (iota((128, WIDE), 1) // C).astype(F32)
            choose = jnp.concatenate(
                [(turned[:, k : k + 1] == of_lane).astype(F32) for k in range(pieces)], axis=0
            ).astype(BF16)
            quads = []
            for k in range(4):
                start, col = k // 2 * quarter, k % 2 * C
                piece = recv[slot, start : start + quarter, col : col + C]
                quads.append(jnp.concatenate([piece] * 4, axis=1))
            masked.append(jnp.concatenate(quads, axis=0) * choose)
        hot = jnp.concatenate(hots, axis=1)
        sums[...] += jnp.dot(hot, jnp.concatenate(masked, axis=0), preferred_element_type=F32)
        counts[...] += lax.dot_general(
            jnp.concatenate(flat_hots, axis=1),
            jnp.concatenate(depth_hots, axis=1),
            NT,
            preferred_element_type=F32,
        )
        return carry

    lax.fori_loop(0, columns // BATCH, bin_group, 0)

    tally = pltpu.einshape("a(bc)->(ab)c", counts[...], b=ZG)
    share = jnp.where(tally > 0.5, 1.0 / jnp.maximum(tally, 1.0), 0.0)
    first = share.astype(BF16)
    rest = share - first.astype(F32)
    second = rest.astype(BF16)
    third_part = (rest - second.astype(F32)).astype(BF16)
    spread = jnp.where(iota((BE, BE * C), 0) == iota((BE, BE * C), 1) // C, 1.0, 0.0).astype(BF16)
    inverse[...] = (
        jnp.dot(first, spread, preferred_element_type=F32)
        + jnp.dot(second, spread, preferred_element_type=F32)
        + jnp.dot(third_part, spread, preferred_element_type=F32)
    )

    keep_y = (link_ref[0, 2] >= 0).astype(F32)
    keep_z = (link_ref[0, 4] >= 0).astype(F32)

    def side_copy(layer, up):
        k = 2 * layer + up
        return pltpu.make_async_remote_copy(
            src_ref=side_out.at[k],
            dst_ref=side_in.at[k],
            send_sem=side_send.at[k],
            recv_sem=side_recv.at[k],
            device_id=(region + 1 if up else region - 1, block),
            device_id_type=MESH,
        )

    def send_sides(layer):
        pl.when(region > 0)(lambda: side_copy(layer, 0).start())
        pl.when(region < regions - 1)(lambda: side_copy(layer, 1).start())

    def receive_sides(layer):
        def put(k, plane):
            groups = [side_in[k, :, z * WIDE : (z + 1) * WIDE].astype(F32) for z in range(ZG)]
            place_plane(field.at[layer], plane, groups, 0.0, 0.0)

        def blank(plane):
            field[layer, :, plane * BE : (plane + 1) * BE, :] = jnp.zeros((3, BE, ZPAD), BF16)

        @pl.when(region > 0)
        def _():
            side_copy(layer, 1).wait_recv()
            put(2 * layer + 1, 0)

        @pl.when(region < regions - 1)
        def _():
            side_copy(layer, 0).wait_recv()
            put(2 * layer, BE + 1)

        pl.when(region == 0)(lambda: blank(0))
        pl.when(region == regions - 1)(lambda: blank(BE + 1))

    def settle_sides(layer):
        pl.when(region > 0)(lambda: side_copy(layer, 0).wait_send())
        pl.when(region < regions - 1)(lambda: side_copy(layer, 1).wait_send())

    def mean_plane(x):
        rows = slice(x * BE, (x + 1) * BE)
        groups = []
        for z in range(ZG):
            total = sums[z * ROWS + x * BE : z * ROWS + (x + 1) * BE, :]
            mean = (total * inverse[rows, z * WIDE : (z + 1) * WIDE]).astype(BF16)
            voxels[rows, z * WIDE : (z + 1) * WIDE] = mean
            groups.append(mean.astype(F32))
        place_plane(field.at[0], x + 1, groups, keep_y, keep_z)

    mean_plane(0)
    mean_plane(BE - 1)
    side_out[0] = voxels[0:BE, :]
    side_out[1] = voxels[ROWS - BE : ROWS, :]
    send_sides(0)
    for x in range(1, BE - 1):
        mean_plane(x)

    def encode(layer, runs, bias, target):
        total = convolve(field.at[layer], wide_two if layer else wide_one, runs)
        start = 0
        for group in range(ZG):
            cols = slice(group * WIDE, (group + 1) * WIDE)
            for p, n in runs:
                rows = slice(p * BE, (p + n) * BE)
                value = total[start : start + n * BE] + bias
                start += n * BE
                if layer:
                    value = value + voxels[rows, cols].astype(F32)
                value = jnp.where(inverse[rows, cols] > 0.0, jnp.maximum(value, 0.0), 0.0)
                target[rows, cols] = value.astype(BF16)

    def place_hidden(x):
        rows = pl.ds(pl.multiple_of(x * BE, BE), BE)
        groups = [hidden[rows, z * WIDE : (z + 1) * WIDE].astype(F32) for z in range(ZG)]
        place_plane(field.at[1], x + 1, groups, keep_y, keep_z)

    bias_one = jnp.concatenate([bone_ref[...]] * 4, axis=1)
    bias_two = jnp.concatenate([btwo_ref[...]] * 4, axis=1)

    middle, ends = [(1, BE - 2)], [(0, 1), (BE - 1, 1)]
    encode(0, middle, bias_one, hidden)
    receive_sides(0)
    encode(0, ends, bias_one, hidden)
    side_out[2] = hidden[0:BE, :]
    side_out[3] = hidden[ROWS - BE : ROWS, :]
    send_sides(1)
    lax.fori_loop(0, BE, lambda x, carry: (place_hidden(x), carry)[1], 0, unroll=UNROLL)
    encode(1, middle, bias_two, out_ref)
    receive_sides(1)
    encode(1, ends, bias_two, out_ref)

    def settle(slot, carry):
        copy_to(slot, block).wait_send()
        return carry

    lax.fori_loop(1, columns, settle, 0)
    settle_sides(0)
    settle_sides(1)


def unfold(flat_ref, out_hbm, tiles, sems):
    copies = []
    step = ROWS // PARTS
    for k in range(PARTS):
        rows = slice(k * step, (k + 1) * step)
        tiles[rows] = pltpu.einshape("a(bc)->abc", flat_ref[rows, :], b=BE)
        copies.append(pltpu.make_async_copy(tiles.at[rows], out_hbm.at[rows], sems.at[k]))
        copies[-1].start()
    for copy in copies:
        copy.wait()


def per_device(
    dims, point_feats, point_block, point_voxel, neighbours, conv_one, bias_one, conv_two, bias_two
):
    regions, columns = dims
    points = point_feats.shape[0]
    quarter = 2 * points // columns // 4
    vmem = pl.BlockSpec(memory_space=pltpu.VMEM)
    smem = pl.BlockSpec(memory_space=pltpu.SMEM)
    hbm = pl.BlockSpec(memory_space=pl.ANY)
    pack = pltpu.VMEM((columns, 2 * quarter + 16, 128), BF16)
    flat = pl.pallas_call(
        functools.partial(body, dims),
        out_shape=jax.ShapeDtypeStruct((ROWS, BE * C), BF16),
        in_specs=[hbm, vmem, hbm, smem, hbm, vmem, hbm, vmem],
        out_specs=vmem,
        scratch_shapes=[
            pltpu.VMEM((C, points), BF16),
            pltpu.VMEM((1, points), jnp.int32),
            pltpu.VMEM((27, C, C), BF16),
            pltpu.VMEM((27, C, C), BF16),
            pltpu.VMEM((WIDE, points), BF16),
            pltpu.VMEM((columns * 16, 128), BF16),
            pack,
            pack,
            pltpu.VMEM((ZG * ROWS, WIDE), F32),
            pltpu.VMEM((64, 64), F32),
            pltpu.VMEM((ROWS, BE * C), F32),
            pltpu.VMEM((ROWS, BE * C), BF16),
            pltpu.VMEM((ROWS, BE * C), BF16),
            pltpu.VMEM((2, 3, (BE + 2) * BE, ZPAD), BF16),
            pltpu.VMEM((9 * TAP, WIDE), BF16),
            pltpu.VMEM((9 * TAP, WIDE), BF16),
            pltpu.VMEM((4, BE, BE * C), BF16),
            pltpu.VMEM((4, BE, BE * C), BF16),
            pltpu.SemaphoreType.DMA((columns,)),
            pltpu.SemaphoreType.DMA((columns,)),
            pltpu.SemaphoreType.DMA((4,)),
            pltpu.SemaphoreType.DMA((4,)),
            pltpu.SemaphoreType.DMA((4,)),
        ],
        compiler_params=pltpu.CompilerParams(
            collective_id=0, has_side_effects=True, vmem_limit_bytes=60 * 2**20
        ),
    )(
        point_feats.T,
        point_block.T,
        point_voxel.reshape(1, points),
        neighbours,
        conv_one,
        bias_one.reshape(1, C),
        conv_two,
        bias_two.reshape(1, C),
    )
    out = pl.pallas_call(
        unfold,
        out_shape=jax.ShapeDtypeStruct((ROWS, BE, C), BF16),
        in_specs=[vmem],
        out_specs=hbm,
        scratch_shapes=[pltpu.VMEM((ROWS, BE, C), BF16), pltpu.SemaphoreType.DMA((PARTS,))],
        compiler_params=pltpu.CompilerParams(vmem_limit_bytes=8 * 2**20),
    )(flat)
    return out.reshape(1, BE, BE, BE, C)


def solution(mesh):
    dims = (mesh.shape["region"], mesh.shape["block"])
    return jax.shard_map(
        functools.partial(per_device, dims),
        mesh=mesh,
        in_specs=(
            P(("region", "block"), None),
            P(("region", "block"), None),
            P(("region", "block")),
            P(("region", "block"), None),
            P(),
            P(),
            P(),
            P(),
        ),
        out_specs=P(("region", "block"), None, None, None, None),
        check_vma=False,
    )
```

```python
import functools
import math

import jax
import jax.numpy as jnp
from jax import lax
from jax.experimental import pallas as pl
from jax.experimental.pallas import tpu as pltpu
from jax.sharding import PartitionSpec as P

BE = 16
C = 64
ROWS = BE * BE
ZG = 4
BATCH = 4
PARTS = 8
UNROLL = 16
WIDE = 4 * C
ZPAD = (BE + 2) * C
TAP = 6 * C
NT = (((1,), (1,)), ((), ()))
F32 = jnp.float32
BF16 = jnp.bfloat16
MESH = pl.DeviceIdType.MESH


def iota(shape, dim):
    return lax.broadcasted_iota(jnp.int32, shape, dim)


def onehot(ids, row):
    return jnp.where(ids == row, jnp.ones((), BF16), jnp.zeros((), BF16))


def ranks_of(blk, columns):
    points = blk.shape[1]
    chunks = points // 256
    member = (iota((columns, points), 0) == blk).astype(F32)
    stacked = jnp.concatenate(
        [member[:, k * 256 : (k + 1) * 256] for k in range(chunks)], axis=0
    ).astype(BF16)
    before = (iota((256, 256), 0) < iota((256, 256), 1)).astype(F32).astype(BF16)
    prefix = jnp.dot(stacked, before, preferred_element_type=F32)
    totals = jnp.dot(stacked, jnp.ones((256, 256), BF16), preferred_element_type=F32)
    running = jnp.zeros((columns, 256), F32)
    rows = []
    for k in range(chunks):
        part = slice(k * columns, (k + 1) * columns)
        own = member[:, k * 256 : (k + 1) * 256]
        rows.append(jnp.sum(own * (prefix[part] + running), axis=0, keepdims=True))
        running = running + totals[part]
    return jnp.concatenate(rows, axis=1)


def build_weights(conv_ref, wide_ref):
    wide_ref[...] = jnp.zeros_like(wide_ref)

    def one(t, carry):
        w0, w1, w2 = conv_ref[3 * t], conv_ref[3 * t + 1], conv_ref[3 * t + 2]
        none = jnp.zeros_like(w0)
        pairs = ((w0, none), (w1, w0), (w2, w1), (none, w2))
        for k, pair in enumerate(pairs):
            tile = jnp.concatenate(pair, axis=1)
            for half in range(2):
                start = pl.multiple_of(t * TAP + (k + 2 * half) * C, C)
                wide_ref[pl.ds(start, C), half * 128 : (half + 1) * 128] = tile
        return carry

    lax.fori_loop(0, 9, one, 0)


def place_plane(field_ref, plane, groups, keep_y, keep_z):
    lane = iota((BE, 128), 1)
    rolled = []
    for group in groups:
        for half in range(2):
            rolled.append(pltpu.roll(group[:, half * 128 : (half + 1) * 128], 64, 1))
    before = [rolled[-1] * keep_z] + rolled
    after = rolled + [rolled[0] * keep_z]
    wide = jnp.concatenate(
        [jnp.where(lane < C, b, a) for b, a in zip(before, after)], axis=1
    )
    row, col = iota((BE, ZPAD), 0), iota((BE, ZPAD), 1)
    inner = ((col >= C) & (col < ZPAD - C)).astype(F32) * keep_y
    down = pltpu.roll(wide, 1, 0)
    down = jnp.where(row == 0, down * inner, down)
    up = pltpu.roll(wide, BE - 1, 0)
    up = jnp.where(row == BE - 1, up * inner, up)
    rows = pl.ds(pl.multiple_of(plane * BE, BE), BE)
    field_ref[0, rows, :] = down.astype(BF16)
    field_ref[1, rows, :] = wide.astype(BF16)
    field_ref[2, rows, :] = up.astype(BF16)


def convolve(field_ref, wide_ref, runs):
    def window(tap, group):
        dx, dy = divmod(tap, 3)
        cols = slice(group * WIDE, group * WIDE + TAP)
        return [field_ref[dy, (p + dx) * BE : (p + dx + n) * BE, cols] for p, n in runs]

    total = None
    for first in range(0, 9, 2):
        taps = [t for t in (first, first + 1) if t < 9]
        columns = [
            jnp.concatenate([part for group in range(ZG) for part in window(t, group)], axis=0)
            for t in taps
        ]
        right = wide_ref[first * TAP : (first + len(taps)) * TAP, :]
        part = jnp.dot(jnp.concatenate(columns, axis=1), right, preferred_element_type=F32)
        total = part if total is None else total + part
    return total


def body(
    dims, feats_hbm, blk_ref, vox_hbm, link_ref, one_hbm, bone_ref, two_hbm, btwo_ref, out_ref,
    feats_ref, vox_ref, one_ref, two_ref,
    expanded, indices, codes_in, send, recv, sums, counts, inverse, voxels, hidden, field, wide_one, wide_two,
    side_out, side_in, send_sem, recv_sem, side_send, side_recv, load_sem, code_send, code_recv,
):
    regions, columns = dims
    side = math.isqrt(columns)
    points = blk_ref.shape[1]
    cap = 2 * points // columns
    quarter = cap // 4
    region, block = lax.axis_index("region"), lax.axis_index("block")
    my_y, my_x = block // side, block % side
    loads = [
        pltpu.make_async_copy(source, target, load_sem.at[k])
        for k, (source, target) in enumerate(
            [(vox_hbm, vox_ref), (feats_hbm, feats_ref), (one_hbm, one_ref), (two_hbm, two_ref)]
        )
    ]
    for load in loads:
        load.start()

    def at(dy, dx):
        return lax.rem(my_y + dy, side) * side + lax.rem(my_x + dx, side)

    barrier = pltpu.get_barrier_semaphore()
    for dy in range(side):
        for dx in range(side):
            if dy or dx:
                pl.semaphore_signal(
                    barrier, inc=1, device_id=(region, at(dy, dx)), device_id_type=MESH
                )

    @pl.when(region > 0)
    def _():
        pl.semaphore_signal(barrier, inc=1, device_id=(region - 1, block), device_id_type=MESH)

    @pl.when(region < regions - 1)
    def _():
        pl.semaphore_signal(barrier, inc=1, device_id=(region + 1, block), device_id_type=MESH)

    blk = blk_ref[...]
    rank = ranks_of(blk, columns)
    low = (
        (rank >= quarter).astype(F32)
        + (rank >= 2 * quarter).astype(F32)
        + (rank >= 3 * quarter).astype(F32)
    )
    high = rank - quarter * low
    loads[0].wait()
    loads[1].wait()
    feats = feats_ref[...]
    for k in range(4):
        expanded[k * C : (k + 1) * C, :] = feats * (low == k).astype(F32).astype(BF16)

    third = (rank >= 128).astype(F32) + (rank >= 256).astype(F32)
    place = (rank - 128 * third).astype(BF16)
    number = vox_ref[...]
    code_a = (number // 64 + 1).astype(F32).astype(BF16)
    code_b = (number % 64).astype(F32).astype(BF16)
    slot_row = (blk.astype(F32) * 8 + third).astype(BF16)
    where_to = onehot(iota((columns * 8, points), 0).astype(F32).astype(BF16), slot_row)
    spots = onehot(iota((128, points), 0).astype(F32).astype(BF16), place)
    codes = jnp.concatenate([spots * code_a, spots * code_b], axis=0)
    coded = lax.dot_general(where_to, codes, NT, preferred_element_type=F32)
    for k in range(columns):
        pair = [coded[k * 8 : (k + 1) * 8, half * 128 : (half + 1) * 128] for half in range(2)]
        indices[k * 16 : (k + 1) * 16, :] = jnp.concatenate(pair, axis=0).astype(BF16)

    arrivals = columns - 1 + (region > 0).astype(jnp.int32) + (region < regions - 1).astype(jnp.int32)
    pl.semaphore_wait(barrier, arrivals)

    def copy_to(slot, target):
        return pltpu.make_async_remote_copy(
            src_ref=send.at[slot],
            dst_ref=recv.at[slot],
            send_sem=send_sem.at[slot],
            recv_sem=recv_sem.at[slot],
            device_id=(region, target),
            device_id_type=MESH,
        )

    def code_copy(slot, target):
        rows = pl.ds(pl.multiple_of(target * 16, 16), 16)
        return pltpu.make_async_remote_copy(
            src_ref=indices.at[rows],
            dst_ref=codes_in.at[slot],
            send_sem=code_send.at[slot],
            recv_sem=code_recv.at[slot],
            device_id=(region, target),
            device_id_type=MESH,
        )

    def send_codes(slot, carry):
        j = lax.rem(slot, side)
        code_copy(slot, at(j, lax.rem(slot // side + j, side))).start()
        return carry

    lax.fori_loop(side, columns, send_codes, 0)
    lax.fori_loop(1, side, send_codes, 0)
    codes_in[0] = indices[pl.ds(pl.multiple_of(block * 16, 16), 16), :]

    def send_group(step, carry):
        turn = lax.rem(step + 1, side)
        targets = [at(j, lax.rem(turn + j, side)) for j in range(side)]
        blocks = blk_ref[...]
        placing = jnp.concatenate(
            [
                onehot(
                    iota((quarter, points), 0).astype(F32).astype(BF16),
                    jnp.where(blocks == target, high, -1.0).astype(BF16),
                )
                for target in targets
            ],
            axis=0,
        )
        packed = lax.dot_general(placing, expanded[...], NT, preferred_element_type=F32)
        packed = packed.astype(BF16)
        for j, target in enumerate(targets):
            slot = turn * side + j
            mine = packed[j * quarter : (j + 1) * quarter]

            def fill(pack):
                pack[slot, 0:quarter, :] = mine[:, 0:128]
                pack[slot, quarter : 2 * quarter, :] = mine[:, 128:256]

            def ship():
                fill(send)
                copy_to(slot, target).start()

            if j == 0:

                pl.when(turn == 0)(lambda: fill(recv))
                pl.when(turn != 0)(ship)
            else:
                ship()
        return carry

    lax.fori_loop(0, side, send_group, 0)

    loads[2].wait()
    build_weights(one_ref, wide_one)
    loads[3].wait()
    build_weights(two_ref, wide_two)

    sums[...] = jnp.zeros_like(sums)
    counts[...] = jnp.zeros_like(counts)

    pieces = cap // 128
    names = iota((ROWS, 128), 0).astype(F32).astype(BF16)

    def slot_at(turn):
        return jnp.where(turn == 0, 0, lax.rem(turn + side - 2, columns - 1) + 1)

    def arrive(copy, turn, first):
        if first:
            pl.when(turn != 0)(lambda: copy(slot_at(turn), block).wait_recv())
        else:
            copy(slot_at(turn), block).wait_recv()

    def count_group(step, carry):
        tables = ([], [])
        for j in range(BATCH):
            turn = step * BATCH + j
            arrive(code_copy, turn, j == 0)
            code = codes_in[slot_at(turn)].astype(F32)
            for table, value in zip(tables, (code[0:8] - 1.0, code[8:16])):
                for k in range(pieces):
                    table.append(onehot(names[:64], value[k : k + 1].astype(BF16)))
        coarse, fine = [jnp.concatenate(table, axis=1) for table in tables]
        counts[...] += lax.dot_general(coarse, fine, NT, preferred_element_type=F32)
        return carry

    lax.fori_loop(0, columns // BATCH, count_group, 0)
    tally = pltpu.einshape("a(bc)->(ab)c", counts[...], b=ZG)
    share = jnp.where(tally > 0.5, 1.0 / jnp.maximum(tally, 1.0), 0.0)
    first = share.astype(BF16)
    rest = share - first.astype(F32)
    second = rest.astype(BF16)
    third_part = (rest - second.astype(F32)).astype(BF16)
    spread = jnp.where(iota((BE, BE * C), 0) == iota((BE, BE * C), 1) // C, 1.0, 0.0).astype(BF16)
    inverse[...] = (
        jnp.dot(first, spread, preferred_element_type=F32)
        + jnp.dot(second, spread, preferred_element_type=F32)
        + jnp.dot(third_part, spread, preferred_element_type=F32)
    )


    def bin_group(base, size):
        hots, masked = [], []
        for j in range(size):
            turn = base + j
            slot = slot_at(turn)
            arrive(copy_to, turn, j == 0)
            code = codes_in[slot].astype(F32)
            a = code[0:8].astype(jnp.int32) - 1
            b = code[8:16].astype(jnp.int32)
            flat = a * 4 + (b >> 4)
            deep = (b >> 2) & 3
            inner = (b & 3).astype(F32)
            flat = flat.astype(F32)
            by_group = []
            for group in range(ZG):
                row = jnp.where(deep == group, flat, -1.0)
                by_group.append(
                    jnp.concatenate(
                        [onehot(names, row[k : k + 1].astype(BF16)) for k in range(pieces)], axis=1
                    )
                )
            hots.append(jnp.concatenate(by_group, axis=0))
            turned = inner.T
            of_lane = (iota((128, WIDE), 1) // C).astype(F32)
            choose = jnp.concatenate(
                [(turned[:, k : k + 1] == of_lane).astype(F32) for k in range(pieces)], axis=0
            ).astype(BF16)
            quads = []
            for k in range(4):
                start, col = k // 2 * quarter, k % 2 * C
                piece = recv[slot, start : start + quarter, col : col + C]
                quads.append(jnp.concatenate([piece] * 4, axis=1))
            masked.append(jnp.concatenate(quads, axis=0) * choose)
        hot = jnp.concatenate(hots, axis=1)
        sums[...] += jnp.dot(hot, jnp.concatenate(masked, axis=0), preferred_element_type=F32)

    lax.fori_loop(
        0, columns // BATCH, lambda step, carry: (bin_group(step * BATCH, BATCH), carry)[1], 0
    )

    keep_y = (link_ref[0, 2] >= 0).astype(F32)
    keep_z = (link_ref[0, 4] >= 0).astype(F32)

    def side_copy(layer, up):
        k = 2 * layer + up
        return pltpu.make_async_remote_copy(
            src_ref=side_out.at[k],
            dst_ref=side_in.at[k],
            send_sem=side_send.at[k],
            recv_sem=side_recv.at[k],
            device_id=(region + 1 if up else region - 1, block),
            device_id_type=MESH,
        )

    def send_sides(layer):
        pl.when(region > 0)(lambda: side_copy(layer, 0).start())
        pl.when(region < regions - 1)(lambda: side_copy(layer, 1).start())

    def receive_sides(layer):
        def put(k, plane):
            groups = [side_in[k, :, z * WIDE : (z + 1) * WIDE].astype(F32) for z in range(ZG)]
            place_plane(field.at[layer], plane, groups, 0.0, 0.0)

        def blank(plane):
            field[layer, :, plane * BE : (plane + 1) * BE, :] = jnp.zeros((3, BE, ZPAD), BF16)

        @pl.when(region > 0)
        def _():
            side_copy(layer, 1).wait_recv()
            put(2 * layer + 1, 0)

        @pl.when(region < regions - 1)
        def _():
            side_copy(layer, 0).wait_recv()
            put(2 * layer, BE + 1)

        pl.when(region == 0)(lambda: blank(0))
        pl.when(region == regions - 1)(lambda: blank(BE + 1))

    def settle_sides(layer):
        pl.when(region > 0)(lambda: side_copy(layer, 0).wait_send())
        pl.when(region < regions - 1)(lambda: side_copy(layer, 1).wait_send())

    def mean_plane(x):
        rows = slice(x * BE, (x + 1) * BE)
        groups = []
        for z in range(ZG):
            total = sums[z * ROWS + x * BE : z * ROWS + (x + 1) * BE, :]
            mean = (total * inverse[rows, z * WIDE : (z + 1) * WIDE]).astype(BF16)
            voxels[rows, z * WIDE : (z + 1) * WIDE] = mean
            groups.append(mean.astype(F32))
        place_plane(field.at[0], x + 1, groups, keep_y, keep_z)

    mean_plane(0)
    mean_plane(BE - 1)
    side_out[0] = voxels[0:BE, :]
    side_out[1] = voxels[ROWS - BE : ROWS, :]
    send_sides(0)
    for x in range(1, BE - 1):
        mean_plane(x)

    def encode(layer, runs, bias, target):
        total = convolve(field.at[layer], wide_two if layer else wide_one, runs)
        start = 0
        for group in range(ZG):
            cols = slice(group * WIDE, (group + 1) * WIDE)
            for p, n in runs:
                rows = slice(p * BE, (p + n) * BE)
                value = total[start : start + n * BE] + bias
                start += n * BE
                if layer:
                    value = value + voxels[rows, cols].astype(F32)
                value = jnp.where(inverse[rows, cols] > 0.0, jnp.maximum(value, 0.0), 0.0)
                target[rows, cols] = value.astype(BF16)

    def place_hidden(x):
        rows = pl.ds(pl.multiple_of(x * BE, BE), BE)
        groups = [hidden[rows, z * WIDE : (z + 1) * WIDE].astype(F32) for z in range(ZG)]
        place_plane(field.at[1], x + 1, groups, keep_y, keep_z)

    bias_one = jnp.concatenate([bone_ref[...]] * 4, axis=1)
    bias_two = jnp.concatenate([btwo_ref[...]] * 4, axis=1)

    middle, ends = [(1, BE - 2)], [(0, 1), (BE - 1, 1)]
    encode(0, middle, bias_one, hidden)
    receive_sides(0)
    encode(0, ends, bias_one, hidden)
    side_out[2] = hidden[0:BE, :]
    side_out[3] = hidden[ROWS - BE : ROWS, :]
    send_sides(1)
    lax.fori_loop(0, BE, lambda x, carry: (place_hidden(x), carry)[1], 0, unroll=UNROLL)
    encode(1, middle, bias_two, out_ref)
    receive_sides(1)
    encode(1, ends, bias_two, out_ref)

    def settle(slot, carry):
        copy_to(slot, block).wait_send()
        code_copy(slot, block).wait_send()
        return carry

    lax.fori_loop(1, columns, settle, 0)
    settle_sides(0)
    settle_sides(1)


def unfold(flat_ref, out_hbm, tiles, sems):
    copies = []
    step = ROWS // PARTS
    for k in range(PARTS):
        rows = slice(k * step, (k + 1) * step)
        tiles[rows] = pltpu.einshape("a(bc)->abc", flat_ref[rows, :], b=BE)
        copies.append(pltpu.make_async_copy(tiles.at[rows], out_hbm.at[rows], sems.at[k]))
        copies[-1].start()
    for copy in copies:
        copy.wait()


def per_device(
    dims, point_feats, point_block, point_voxel, neighbours, conv_one, bias_one, conv_two, bias_two
):
    regions, columns = dims
    points = point_feats.shape[0]
    quarter = 2 * points // columns // 4
    vmem = pl.BlockSpec(memory_space=pltpu.VMEM)
    smem = pl.BlockSpec(memory_space=pltpu.SMEM)
    hbm = pl.BlockSpec(memory_space=pl.ANY)
    pack = pltpu.VMEM((columns, 2 * quarter, 128), BF16)
    flat = pl.pallas_call(
        functools.partial(body, dims),
        out_shape=jax.ShapeDtypeStruct((ROWS, BE * C), BF16),
        in_specs=[hbm, vmem, hbm, smem, hbm, vmem, hbm, vmem],
        out_specs=vmem,
        scratch_shapes=[
            pltpu.VMEM((C, points), BF16),
            pltpu.VMEM((1, points), jnp.int32),
            pltpu.VMEM((27, C, C), BF16),
            pltpu.VMEM((27, C, C), BF16),
            pltpu.VMEM((WIDE, points), BF16),
            pltpu.VMEM((columns * 16, 128), BF16),
            pltpu.VMEM((columns, 16, 128), BF16),
            pack,
            pack,
            pltpu.VMEM((ZG * ROWS, WIDE), F32),
            pltpu.VMEM((64, 64), F32),
            pltpu.VMEM((ROWS, BE * C), F32),
            pltpu.VMEM((ROWS, BE * C), BF16),
            pltpu.VMEM((ROWS, BE * C), BF16),
            pltpu.VMEM((2, 3, (BE + 2) * BE, ZPAD), BF16),
            pltpu.VMEM((9 * TAP, WIDE), BF16),
            pltpu.VMEM((9 * TAP, WIDE), BF16),
            pltpu.VMEM((4, BE, BE * C), BF16),
            pltpu.VMEM((4, BE, BE * C), BF16),
            pltpu.SemaphoreType.DMA((columns,)),
            pltpu.SemaphoreType.DMA((columns,)),
            pltpu.SemaphoreType.DMA((4,)),
            pltpu.SemaphoreType.DMA((4,)),
            pltpu.SemaphoreType.DMA((4,)),
            pltpu.SemaphoreType.DMA((columns,)),
            pltpu.SemaphoreType.DMA((columns,)),
        ],
        compiler_params=pltpu.CompilerParams(
            collective_id=0, has_side_effects=True, vmem_limit_bytes=60 * 2**20
        ),
    )(
        point_feats.T,
        point_block.T,
        point_voxel.reshape(1, points),
        neighbours,
        conv_one,
        bias_one.reshape(1, C),
        conv_two,
        bias_two.reshape(1, C),
    )
    out = pl.pallas_call(
        unfold,
        out_shape=jax.ShapeDtypeStruct((ROWS, BE, C), BF16),
        in_specs=[vmem],
        out_specs=hbm,
        scratch_shapes=[pltpu.VMEM((ROWS, BE, C), BF16), pltpu.SemaphoreType.DMA((PARTS,))],
        compiler_params=pltpu.CompilerParams(vmem_limit_bytes=8 * 2**20),
    )(flat)
    return out.reshape(1, BE, BE, BE, C)


def solution(mesh):
    dims = (mesh.shape["region"], mesh.shape["block"])
    return jax.shard_map(
        functools.partial(per_device, dims),
        mesh=mesh,
        in_specs=(
            P(("region", "block"), None),
            P(("region", "block"), None),
            P(("region", "block")),
            P(("region", "block"), None),
            P(),
            P(),
            P(),
            P(),
        ),
        out_specs=P(("region", "block"), None, None, None, None),
        check_vma=False,
    )
```

```python
import functools
import math

import jax
import jax.numpy as jnp
from jax import lax
from jax.experimental import pallas as pl
from jax.experimental.pallas import tpu as pltpu
from jax.sharding import PartitionSpec as P

BE = 16
C = 64
ROWS = BE * BE
ZG = 4
BATCH = 4
PARTS = 8
UNROLL = 16
WIDE = 4 * C
ZPAD = (BE + 2) * C
TAP = 6 * C
NT = (((1,), (1,)), ((), ()))
F32 = jnp.float32
BF16 = jnp.bfloat16
MESH = pl.DeviceIdType.MESH


def iota(shape, dim):
    return lax.broadcasted_iota(jnp.int32, shape, dim)


def onehot(ids, row):
    return jnp.where(ids == row, jnp.ones((), BF16), jnp.zeros((), BF16))


def ranks_of(blk, columns):
    points = blk.shape[1]
    chunks = points // 256
    member = (iota((columns, points), 0) == blk).astype(F32)
    stacked = jnp.concatenate(
        [member[:, k * 256 : (k + 1) * 256] for k in range(chunks)], axis=0
    ).astype(BF16)
    before = (iota((256, 256), 0) < iota((256, 256), 1)).astype(F32).astype(BF16)
    prefix = jnp.dot(stacked, before, preferred_element_type=F32)
    totals = jnp.dot(stacked, jnp.ones((256, 256), BF16), preferred_element_type=F32)
    running = jnp.zeros((columns, 256), F32)
    rows = []
    for k in range(chunks):
        part = slice(k * columns, (k + 1) * columns)
        own = member[:, k * 256 : (k + 1) * 256]
        rows.append(jnp.sum(own * (prefix[part] + running), axis=0, keepdims=True))
        running = running + totals[part]
    return jnp.concatenate(rows, axis=1)


def build_weights(conv_ref, wide_ref):
    wide_ref[...] = jnp.zeros_like(wide_ref)

    def one(t, carry):
        w0, w1, w2 = conv_ref[3 * t], conv_ref[3 * t + 1], conv_ref[3 * t + 2]
        none = jnp.zeros_like(w0)
        pairs = ((w0, none), (w1, w0), (w2, w1), (none, w2))
        for k, pair in enumerate(pairs):
            tile = jnp.concatenate(pair, axis=1)
            for half in range(2):
                start = pl.multiple_of(t * TAP + (k + 2 * half) * C, C)
                wide_ref[pl.ds(start, C), half * 128 : (half + 1) * 128] = tile
        return carry

    lax.fori_loop(0, 9, one, 0)


def place_plane(field_ref, plane, groups, keep_y, keep_z):
    lane = iota((BE, 128), 1)
    rolled = []
    for group in groups:
        for half in range(2):
            rolled.append(pltpu.roll(group[:, half * 128 : (half + 1) * 128], 64, 1))
    before = [rolled[-1] * keep_z] + rolled
    after = rolled + [rolled[0] * keep_z]
    wide = jnp.concatenate(
        [jnp.where(lane < C, b, a) for b, a in zip(before, after)], axis=1
    )
    row, col = iota((BE, ZPAD), 0), iota((BE, ZPAD), 1)
    inner = ((col >= C) & (col < ZPAD - C)).astype(F32) * keep_y
    down = pltpu.roll(wide, 1, 0)
    down = jnp.where(row == 0, down * inner, down)
    up = pltpu.roll(wide, BE - 1, 0)
    up = jnp.where(row == BE - 1, up * inner, up)
    rows = pl.ds(pl.multiple_of(plane * BE, BE), BE)
    field_ref[0, rows, :] = down.astype(BF16)
    field_ref[1, rows, :] = wide.astype(BF16)
    field_ref[2, rows, :] = up.astype(BF16)


def convolve(field_ref, wide_ref, runs):
    def window(tap, group):
        dx, dy = divmod(tap, 3)
        cols = slice(group * WIDE, group * WIDE + TAP)
        return [field_ref[dy, (p + dx) * BE : (p + dx + n) * BE, cols] for p, n in runs]

    total = None
    for first in range(0, 9, 2):
        taps = [t for t in (first, first + 1) if t < 9]
        columns = [
            jnp.concatenate([part for group in range(ZG) for part in window(t, group)], axis=0)
            for t in taps
        ]
        right = wide_ref[first * TAP : (first + len(taps)) * TAP, :]
        part = jnp.dot(jnp.concatenate(columns, axis=1), right, preferred_element_type=F32)
        total = part if total is None else total + part
    return total


def body(
    dims, feats_hbm, blk_ref, vox_hbm, link_ref, one_hbm, bone_ref, two_hbm, btwo_ref, out_hbm,
    feats_ref, vox_ref, one_ref, two_ref,
    expanded, indices, codes_in, send, recv, sums, counts, inverse, voxels, hidden, field, wide_one, wide_two,
    side_out, side_in, send_sem, recv_sem, side_send, side_recv, load_sem, code_send, code_recv, result, save_sem,
):
    regions, columns = dims
    side = math.isqrt(columns)
    points = blk_ref.shape[1]
    cap = 2 * points // columns
    quarter = cap // 4
    region, block = lax.axis_index("region"), lax.axis_index("block")
    my_y, my_x = block // side, block % side
    loads = [
        pltpu.make_async_copy(source, target, load_sem.at[k])
        for k, (source, target) in enumerate(
            [(vox_hbm, vox_ref), (feats_hbm, feats_ref), (one_hbm, one_ref), (two_hbm, two_ref)]
        )
    ]
    for load in loads:
        load.start()

    def at(dy, dx):
        return lax.rem(my_y + dy, side) * side + lax.rem(my_x + dx, side)

    barrier = pltpu.get_barrier_semaphore()
    for dy in range(side):
        for dx in range(side):
            if dy or dx:
                pl.semaphore_signal(
                    barrier, inc=1, device_id=(region, at(dy, dx)), device_id_type=MESH
                )

    @pl.when(region > 0)
    def _():
        pl.semaphore_signal(barrier, inc=1, device_id=(region - 1, block), device_id_type=MESH)

    @pl.when(region < regions - 1)
    def _():
        pl.semaphore_signal(barrier, inc=1, device_id=(region + 1, block), device_id_type=MESH)

    blk = blk_ref[...]
    rank = ranks_of(blk, columns)
    low = (
        (rank >= quarter).astype(F32)
        + (rank >= 2 * quarter).astype(F32)
        + (rank >= 3 * quarter).astype(F32)
    )
    high = rank - quarter * low
    loads[0].wait()
    loads[1].wait()
    feats = feats_ref[...]
    for k in range(4):
        expanded[k * C : (k + 1) * C, :] = feats * (low == k).astype(F32).astype(BF16)

    third = (rank >= 128).astype(F32) + (rank >= 256).astype(F32)
    place = (rank - 128 * third).astype(BF16)
    number = vox_ref[...]
    code_a = (number // 64 + 1).astype(F32).astype(BF16)
    code_b = (number % 64).astype(F32).astype(BF16)
    slot_row = (blk.astype(F32) * 8 + third).astype(BF16)
    where_to = onehot(iota((columns * 8, points), 0).astype(F32).astype(BF16), slot_row)
    spots = onehot(iota((128, points), 0).astype(F32).astype(BF16), place)
    codes = jnp.concatenate([spots * code_a, spots * code_b], axis=0)
    coded = lax.dot_general(where_to, codes, NT, preferred_element_type=F32)
    for k in range(columns):
        pair = [coded[k * 8 : (k + 1) * 8, half * 128 : (half + 1) * 128] for half in range(2)]
        indices[k * 16 : (k + 1) * 16, :] = jnp.concatenate(pair, axis=0).astype(BF16)

    arrivals = columns - 1 + (region > 0).astype(jnp.int32) + (region < regions - 1).astype(jnp.int32)
    pl.semaphore_wait(barrier, arrivals)

    def copy_to(slot, target):
        return pltpu.make_async_remote_copy(
            src_ref=send.at[slot],
            dst_ref=recv.at[slot],
            send_sem=send_sem.at[slot],
            recv_sem=recv_sem.at[slot],
            device_id=(region, target),
            device_id_type=MESH,
        )

    def code_copy(slot, target):
        rows = pl.ds(pl.multiple_of(target * 16, 16), 16)
        return pltpu.make_async_remote_copy(
            src_ref=indices.at[rows],
            dst_ref=codes_in.at[slot],
            send_sem=code_send.at[slot],
            recv_sem=code_recv.at[slot],
            device_id=(region, target),
            device_id_type=MESH,
        )

    def send_codes(slot, carry):
        j = lax.rem(slot, side)
        code_copy(slot, at(j, lax.rem(slot // side + j, side))).start()
        return carry

    lax.fori_loop(side, columns, send_codes, 0)
    lax.fori_loop(1, side, send_codes, 0)
    codes_in[0] = indices[pl.ds(pl.multiple_of(block * 16, 16), 16), :]

    def send_group(step, carry):
        turns = [lax.rem(2 * step + 1 + q, side) for q in range(2)]
        places = [(turn, j) for turn in turns for j in range(side)]
        targets = [at(j, lax.rem(turn + j, side)) for turn, j in places]
        blocks = blk_ref[...]
        placing = jnp.concatenate(
            [
                onehot(
                    iota((quarter, points), 0).astype(F32).astype(BF16),
                    jnp.where(blocks == target, high, -1.0).astype(BF16),
                )
                for target in targets
            ],
            axis=0,
        )
        packed = lax.dot_general(placing, expanded[...], NT, preferred_element_type=F32)
        packed = packed.astype(BF16)
        for k, target in enumerate(targets):
            turn, j = places[k]
            slot = turn * side + j
            mine = packed[k * quarter : (k + 1) * quarter]

            def fill(pack):
                pack[slot, 0:quarter, :] = mine[:, 0:128]
                pack[slot, quarter : 2 * quarter, :] = mine[:, 128:256]

            def ship():
                fill(send)
                copy_to(slot, target).start()

            if j == 0:

                pl.when(turn == 0)(lambda: fill(recv))
                pl.when(turn != 0)(ship)
            else:
                ship()
        return carry

    lax.fori_loop(0, side // 2, send_group, 0)

    loads[2].wait()
    build_weights(one_ref, wide_one)
    loads[3].wait()
    build_weights(two_ref, wide_two)

    sums[...] = jnp.zeros_like(sums)
    counts[...] = jnp.zeros_like(counts)

    pieces = cap // 128
    names = iota((ROWS, 128), 0).astype(F32).astype(BF16)

    def slot_at(turn):
        return jnp.where(turn == 0, 0, lax.rem(turn + side - 2, columns - 1) + 1)

    def arrive(copy, turn, first):
        if first:
            pl.when(turn != 0)(lambda: copy(slot_at(turn), block).wait_recv())
        else:
            copy(slot_at(turn), block).wait_recv()

    def count_group(step, carry):
        tables = ([], [])
        for j in range(BATCH):
            turn = step * BATCH + j
            arrive(code_copy, turn, j == 0)
            code = codes_in[slot_at(turn)].astype(F32)
            for table, value in zip(tables, (code[0:8] - 1.0, code[8:16])):
                for k in range(pieces):
                    table.append(onehot(names[:64], value[k : k + 1].astype(BF16)))
        coarse, fine = [jnp.concatenate(table, axis=1) for table in tables]
        counts[...] += lax.dot_general(coarse, fine, NT, preferred_element_type=F32)
        return carry

    lax.fori_loop(0, columns // BATCH, count_group, 0)
    tally = pltpu.einshape("a(bc)->(ab)c", counts[...], b=ZG)
    share = jnp.where(tally > 0.5, 1.0 / jnp.maximum(tally, 1.0), 0.0)
    first = share.astype(BF16)
    rest = share - first.astype(F32)
    second = rest.astype(BF16)
    third_part = (rest - second.astype(F32)).astype(BF16)
    spread = jnp.where(iota((BE, BE * C), 0) == iota((BE, BE * C), 1) // C, 1.0, 0.0).astype(BF16)
    inverse[...] = (
        jnp.dot(first, spread, preferred_element_type=F32)
        + jnp.dot(second, spread, preferred_element_type=F32)
        + jnp.dot(third_part, spread, preferred_element_type=F32)
    )


    def bin_group(base, size):
        hots, masked = [], []
        for j in range(size):
            turn = base + j
            slot = slot_at(turn)
            arrive(copy_to, turn, j == 0)
            code = codes_in[slot].astype(F32)
            a = code[0:8].astype(jnp.int32) - 1
            b = code[8:16].astype(jnp.int32)
            flat = a * 4 + (b >> 4)
            deep = (b >> 2) & 3
            inner = (b & 3).astype(F32)
            flat = flat.astype(F32)
            by_group = []
            for group in range(ZG):
                row = jnp.where(deep == group, flat, -1.0)
                by_group.append(
                    jnp.concatenate(
                        [onehot(names, row[k : k + 1].astype(BF16)) for k in range(pieces)], axis=1
                    )
                )
            hots.append(jnp.concatenate(by_group, axis=0))
            turned = inner.T
            of_lane = (iota((128, WIDE), 1) // C).astype(F32)
            choose = jnp.concatenate(
                [(turned[:, k : k + 1] == of_lane).astype(F32) for k in range(pieces)], axis=0
            ).astype(BF16)
            quads = []
            for k in range(4):
                start, col = k // 2 * quarter, k % 2 * C
                piece = recv[slot, start : start + quarter, col : col + C]
                quads.append(jnp.concatenate([piece] * 4, axis=1))
            masked.append(jnp.concatenate(quads, axis=0) * choose)
        hot = jnp.concatenate(hots, axis=1)
        sums[...] += jnp.dot(hot, jnp.concatenate(masked, axis=0), preferred_element_type=F32)

    lax.fori_loop(
        0, columns // BATCH, lambda step, carry: (bin_group(step * BATCH, BATCH), carry)[1], 0
    )

    keep_y = (link_ref[0, 2] >= 0).astype(F32)
    keep_z = (link_ref[0, 4] >= 0).astype(F32)

    def side_copy(layer, up):
        k = 2 * layer + up
        return pltpu.make_async_remote_copy(
            src_ref=side_out.at[k],
            dst_ref=side_in.at[k],
            send_sem=side_send.at[k],
            recv_sem=side_recv.at[k],
            device_id=(region + 1 if up else region - 1, block),
            device_id_type=MESH,
        )

    def send_sides(layer):
        pl.when(region > 0)(lambda: side_copy(layer, 0).start())
        pl.when(region < regions - 1)(lambda: side_copy(layer, 1).start())

    def receive_sides(layer):
        def put(k, plane):
            groups = [side_in[k, :, z * WIDE : (z + 1) * WIDE].astype(F32) for z in range(ZG)]
            place_plane(field.at[layer], plane, groups, 0.0, 0.0)

        def blank(plane):
            field[layer, :, plane * BE : (plane + 1) * BE, :] = jnp.zeros((3, BE, ZPAD), BF16)

        @pl.when(region > 0)
        def _():
            side_copy(layer, 1).wait_recv()
            put(2 * layer + 1, 0)

        @pl.when(region < regions - 1)
        def _():
            side_copy(layer, 0).wait_recv()
            put(2 * layer, BE + 1)

        pl.when(region == 0)(lambda: blank(0))
        pl.when(region == regions - 1)(lambda: blank(BE + 1))

    def settle_sides(layer):
        pl.when(region > 0)(lambda: side_copy(layer, 0).wait_send())
        pl.when(region < regions - 1)(lambda: side_copy(layer, 1).wait_send())

    def mean_plane(x):
        rows = slice(x * BE, (x + 1) * BE)
        groups = []
        for z in range(ZG):
            total = sums[z * ROWS + x * BE : z * ROWS + (x + 1) * BE, :]
            mean = (total * inverse[rows, z * WIDE : (z + 1) * WIDE]).astype(BF16)
            voxels[rows, z * WIDE : (z + 1) * WIDE] = mean
            groups.append(mean.astype(F32))
        place_plane(field.at[0], x + 1, groups, keep_y, keep_z)

    mean_plane(0)
    mean_plane(BE - 1)
    side_out[0] = voxels[0:BE, :]
    side_out[1] = voxels[ROWS - BE : ROWS, :]
    send_sides(0)
    for x in range(1, BE - 1):
        mean_plane(x)

    def encode(layer, runs, bias, target):
        total = convolve(field.at[layer], wide_two if layer else wide_one, runs)
        start = 0
        for group in range(ZG):
            cols = slice(group * WIDE, (group + 1) * WIDE)
            for p, n in runs:
                rows = slice(p * BE, (p + n) * BE)
                value = total[start : start + n * BE] + bias
                start += n * BE
                if layer:
                    value = value + voxels[rows, cols].astype(F32)
                value = jnp.where(inverse[rows, cols] > 0.0, jnp.maximum(value, 0.0), 0.0)
                target[rows, cols] = value.astype(BF16)

    def place_hidden(x):
        rows = pl.ds(pl.multiple_of(x * BE, BE), BE)
        groups = [hidden[rows, z * WIDE : (z + 1) * WIDE].astype(F32) for z in range(ZG)]
        place_plane(field.at[1], x + 1, groups, keep_y, keep_z)

    bias_one = jnp.concatenate([bone_ref[...]] * 4, axis=1)
    bias_two = jnp.concatenate([btwo_ref[...]] * 4, axis=1)

    middle, ends = [(1, BE - 2)], [(0, 1), (BE - 1, 1)]
    encode(0, middle, bias_one, hidden)
    receive_sides(0)
    encode(0, ends, bias_one, hidden)
    side_out[2] = hidden[0:BE, :]
    side_out[3] = hidden[ROWS - BE : ROWS, :]
    send_sides(1)
    lax.fori_loop(0, BE, lambda x, carry: (place_hidden(x), carry)[1], 0, unroll=UNROLL)
    spans = [slice(BE, ROWS - BE), slice(0, BE), slice(ROWS - BE, ROWS)]
    saves = [
        pltpu.make_async_copy(result.at[rows], out_hbm.at[rows], save_sem.at[k])
        for k, rows in enumerate(spans)
    ]
    encode(1, middle, bias_two, result)
    saves[0].start()
    receive_sides(1)
    encode(1, ends, bias_two, result)
    saves[1].start()
    saves[2].start()

    def settle(slot, carry):
        copy_to(slot, block).wait_send()
        code_copy(slot, block).wait_send()
        return carry

    lax.fori_loop(1, columns, settle, 0)
    settle_sides(0)
    settle_sides(1)
    for save in saves:
        save.wait()


def unfold(flat_ref, out_hbm, tiles, sems):
    copies = []
    step = ROWS // PARTS
    for k in range(PARTS):
        rows = slice(k * step, (k + 1) * step)
        tiles[rows] = pltpu.einshape("a(bc)->abc", flat_ref[rows, :], b=BE)
        copies.append(pltpu.make_async_copy(tiles.at[rows], out_hbm.at[rows], sems.at[k]))
        copies[-1].start()
    for copy in copies:
        copy.wait()


def per_device(
    dims, point_feats, point_block, point_voxel, neighbours, conv_one, bias_one, conv_two, bias_two
):
    regions, columns = dims
    points = point_feats.shape[0]
    quarter = 2 * points // columns // 4
    vmem = pl.BlockSpec(memory_space=pltpu.VMEM)
    smem = pl.BlockSpec(memory_space=pltpu.SMEM)
    hbm = pl.BlockSpec(memory_space=pl.ANY)
    pack = pltpu.VMEM((columns, 2 * quarter, 128), BF16)
    flat = pl.pallas_call(
        functools.partial(body, dims),
        out_shape=jax.ShapeDtypeStruct((ROWS, BE * C), BF16),
        in_specs=[hbm, vmem, hbm, smem, hbm, vmem, hbm, vmem],
        out_specs=hbm,
        scratch_shapes=[
            pltpu.VMEM((C, points), BF16),
            pltpu.VMEM((1, points), jnp.int32),
            pltpu.VMEM((27, C, C), BF16),
            pltpu.VMEM((27, C, C), BF16),
            pltpu.VMEM((WIDE, points), BF16),
            pltpu.VMEM((columns * 16, 128), BF16),
            pltpu.VMEM((columns, 16, 128), BF16),
            pack,
            pack,
            pltpu.VMEM((ZG * ROWS, WIDE), F32),
            pltpu.VMEM((64, 64), F32),
            pltpu.VMEM((ROWS, BE * C), F32),
            pltpu.VMEM((ROWS, BE * C), BF16),
            pltpu.VMEM((ROWS, BE * C), BF16),
            pltpu.VMEM((2, 3, (BE + 2) * BE, ZPAD), BF16),
            pltpu.VMEM((9 * TAP, WIDE), BF16),
            pltpu.VMEM((9 * TAP, WIDE), BF16),
            pltpu.VMEM((4, BE, BE * C), BF16),
            pltpu.VMEM((4, BE, BE * C), BF16),
            pltpu.SemaphoreType.DMA((columns,)),
            pltpu.SemaphoreType.DMA((columns,)),
            pltpu.SemaphoreType.DMA((4,)),
            pltpu.SemaphoreType.DMA((4,)),
            pltpu.SemaphoreType.DMA((4,)),
            pltpu.SemaphoreType.DMA((columns,)),
            pltpu.SemaphoreType.DMA((columns,)),
            pltpu.VMEM((ROWS, BE * C), BF16),
            pltpu.SemaphoreType.DMA((3,)),
        ],
        compiler_params=pltpu.CompilerParams(
            collective_id=0, has_side_effects=True, vmem_limit_bytes=60 * 2**20
        ),
    )(
        point_feats.T,
        point_block.T,
        point_voxel.reshape(1, points),
        neighbours,
        conv_one,
        bias_one.reshape(1, C),
        conv_two,
        bias_two.reshape(1, C),
    )
    out = pl.pallas_call(
        unfold,
        out_shape=jax.ShapeDtypeStruct((ROWS, BE, C), BF16),
        in_specs=[vmem],
        out_specs=hbm,
        scratch_shapes=[pltpu.VMEM((ROWS, BE, C), BF16), pltpu.SemaphoreType.DMA((PARTS,))],
        compiler_params=pltpu.CompilerParams(vmem_limit_bytes=8 * 2**20),
    )(flat)
    return out.reshape(1, BE, BE, BE, C)


def solution(mesh):
    dims = (mesh.shape["region"], mesh.shape["block"])
    return jax.shard_map(
        functools.partial(per_device, dims),
        mesh=mesh,
        in_specs=(
            P(("region", "block"), None),
            P(("region", "block"), None),
            P(("region", "block")),
            P(("region", "block"), None),
            P(),
            P(),
            P(),
            P(),
        ),
        out_specs=P(("region", "block"), None, None, None, None),
        check_vma=False,
    )
```

```python
import functools
import math

import jax
import jax.numpy as jnp
from jax import lax
from jax.experimental import pallas as pl
from jax.experimental.pallas import tpu as pltpu
from jax.sharding import PartitionSpec as P

BE = 16
C = 64
ROWS = BE * BE
ZG = 4
BATCH = 4
PARTS = 8
UNROLL = 16
WIDE = 4 * C
ZPAD = (BE + 2) * C
TAP = 6 * C
NT = (((1,), (1,)), ((), ()))
F32 = jnp.float32
BF16 = jnp.bfloat16
MESH = pl.DeviceIdType.MESH


def iota(shape, dim):
    return lax.broadcasted_iota(jnp.int32, shape, dim)


def onehot(ids, row):
    return jnp.where(ids == row, jnp.ones((), BF16), jnp.zeros((), BF16))


def ranks_of(blk, columns):
    points = blk.shape[1]
    chunks = points // 256
    member = (iota((columns, points), 0) == blk).astype(F32)
    stacked = jnp.concatenate(
        [member[:, k * 256 : (k + 1) * 256] for k in range(chunks)], axis=0
    ).astype(BF16)
    before = (iota((256, 256), 0) < iota((256, 256), 1)).astype(F32).astype(BF16)
    prefix = jnp.dot(stacked, before, preferred_element_type=F32)
    totals = jnp.dot(stacked, jnp.ones((256, 256), BF16), preferred_element_type=F32)
    running = jnp.zeros((columns, 256), F32)
    rows = []
    for k in range(chunks):
        part = slice(k * columns, (k + 1) * columns)
        own = member[:, k * 256 : (k + 1) * 256]
        rows.append(jnp.sum(own * (prefix[part] + running), axis=0, keepdims=True))
        running = running + totals[part]
    return jnp.concatenate(rows, axis=1)


def build_weights(conv_ref, wide_ref):
    wide_ref[...] = jnp.zeros_like(wide_ref)

    def one(t, carry):
        w0, w1, w2 = conv_ref[3 * t], conv_ref[3 * t + 1], conv_ref[3 * t + 2]
        none = jnp.zeros_like(w0)
        pairs = ((w0, none), (w1, w0), (w2, w1), (none, w2))
        for k, pair in enumerate(pairs):
            tile = jnp.concatenate(pair, axis=1)
            for half in range(2):
                start = pl.multiple_of(t * TAP + (k + 2 * half) * C, C)
                wide_ref[pl.ds(start, C), half * 128 : (half + 1) * 128] = tile
        return carry

    lax.fori_loop(0, 9, one, 0)


def place_plane(field_ref, plane, groups, keep_y, keep_z):
    lane = iota((BE, 128), 1)
    rolled = []
    for group in groups:
        for half in range(2):
            rolled.append(pltpu.roll(group[:, half * 128 : (half + 1) * 128], 64, 1))
    before = [rolled[-1] * keep_z] + rolled
    after = rolled + [rolled[0] * keep_z]
    wide = jnp.concatenate(
        [jnp.where(lane < C, b, a) for b, a in zip(before, after)], axis=1
    )
    row, col = iota((BE, ZPAD), 0), iota((BE, ZPAD), 1)
    inner = ((col >= C) & (col < ZPAD - C)).astype(F32) * keep_y
    down = pltpu.roll(wide, 1, 0)
    down = jnp.where(row == 0, down * inner, down)
    up = pltpu.roll(wide, BE - 1, 0)
    up = jnp.where(row == BE - 1, up * inner, up)
    rows = pl.ds(pl.multiple_of(plane * BE, BE), BE)
    field_ref[0, rows, :] = down.astype(BF16)
    field_ref[1, rows, :] = wide.astype(BF16)
    field_ref[2, rows, :] = up.astype(BF16)


def convolve(field_ref, wide_ref, runs):
    def window(tap, group):
        dx, dy = divmod(tap, 3)
        cols = slice(group * WIDE, group * WIDE + TAP)
        return [field_ref[dy, (p + dx) * BE : (p + dx + n) * BE, cols] for p, n in runs]

    total = None
    for first in range(0, 9, 2):
        taps = [t for t in (first, first + 1) if t < 9]
        columns = [
            jnp.concatenate([part for group in range(ZG) for part in window(t, group)], axis=0)
            for t in taps
        ]
        right = wide_ref[first * TAP : (first + len(taps)) * TAP, :]
        part = jnp.dot(jnp.concatenate(columns, axis=1), right, preferred_element_type=F32)
        total = part if total is None else total + part
    return total


def body(
    dims, feats_hbm, blk_ref, vox_hbm, link_ref, one_hbm, bone_ref, two_hbm, btwo_ref, out_hbm,
    feats_ref, vox_ref, one_ref, two_ref,
    expanded, indices, codes_in, send, recv, sums, counts, inverse, voxels, hidden, field, wide_one, wide_two,
    side_in, send_sem, recv_sem, side_send, side_recv, load_sem, code_send, code_recv, result, save_sem,
):
    regions, columns = dims
    side = math.isqrt(columns)
    points = blk_ref.shape[1]
    cap = 2 * points // columns
    quarter = cap // 4
    region, block = lax.axis_index("region"), lax.axis_index("block")
    my_y, my_x = block // side, block % side
    loads = [
        pltpu.make_async_copy(source, target, load_sem.at[k])
        for k, (source, target) in enumerate(
            [(vox_hbm, vox_ref), (feats_hbm, feats_ref), (one_hbm, one_ref), (two_hbm, two_ref)]
        )
    ]
    for load in loads:
        load.start()

    def at(dy, dx):
        return lax.rem(my_y + dy, side) * side + lax.rem(my_x + dx, side)

    barrier = pltpu.get_barrier_semaphore()
    for dy in range(side):
        for dx in range(side):
            if dy or dx:
                pl.semaphore_signal(
                    barrier, inc=1, device_id=(region, at(dy, dx)), device_id_type=MESH
                )

    @pl.when(region > 0)
    def _():
        pl.semaphore_signal(barrier, inc=1, device_id=(region - 1, block), device_id_type=MESH)

    @pl.when(region < regions - 1)
    def _():
        pl.semaphore_signal(barrier, inc=1, device_id=(region + 1, block), device_id_type=MESH)

    blk = blk_ref[...]
    rank = ranks_of(blk, columns)
    low = (
        (rank >= quarter).astype(F32)
        + (rank >= 2 * quarter).astype(F32)
        + (rank >= 3 * quarter).astype(F32)
    )
    high = rank - quarter * low
    loads[0].wait()
    loads[1].wait()
    feats = feats_ref[...]
    for k in range(4):
        expanded[k * C : (k + 1) * C, :] = feats * (low == k).astype(F32).astype(BF16)

    third = (rank >= 128).astype(F32) + (rank >= 256).astype(F32)
    place = (rank - 128 * third).astype(BF16)
    number = vox_ref[...]
    code_a = (number // 64 + 1).astype(F32).astype(BF16)
    code_b = (number % 64).astype(F32).astype(BF16)
    slot_row = (blk.astype(F32) * 8 + third).astype(BF16)
    where_to = onehot(iota((columns * 8, points), 0).astype(F32).astype(BF16), slot_row)
    spots = onehot(iota((128, points), 0).astype(F32).astype(BF16), place)
    codes = jnp.concatenate([spots * code_a, spots * code_b], axis=0)
    coded = lax.dot_general(where_to, codes, NT, preferred_element_type=F32)
    for k in range(columns):
        pair = [coded[k * 8 : (k + 1) * 8, half * 128 : (half + 1) * 128] for half in range(2)]
        indices[k * 16 : (k + 1) * 16, :] = jnp.concatenate(pair, axis=0).astype(BF16)

    arrivals = columns - 1 + (region > 0).astype(jnp.int32) + (region < regions - 1).astype(jnp.int32)
    pl.semaphore_wait(barrier, arrivals)

    def copy_to(slot, target):
        return pltpu.make_async_remote_copy(
            src_ref=send.at[slot],
            dst_ref=recv.at[slot],
            send_sem=send_sem.at[slot],
            recv_sem=recv_sem.at[slot],
            device_id=(region, target),
            device_id_type=MESH,
        )

    def code_copy(slot, target):
        rows = pl.ds(pl.multiple_of(target * 16, 16), 16)
        return pltpu.make_async_remote_copy(
            src_ref=indices.at[rows],
            dst_ref=codes_in.at[slot],
            send_sem=code_send.at[slot],
            recv_sem=code_recv.at[slot],
            device_id=(region, target),
            device_id_type=MESH,
        )

    def send_codes(slot, carry):
        j = lax.rem(slot, side)
        code_copy(slot, at(j, lax.rem(slot // side + j, side))).start()
        return carry

    lax.fori_loop(side, columns, send_codes, 0)
    lax.fori_loop(1, side, send_codes, 0)
    codes_in[0] = indices[pl.ds(pl.multiple_of(block * 16, 16), 16), :]

    def send_group(step, carry):
        turns = [lax.rem(2 * step + 1 + q, side) for q in range(2)]
        places = [(turn, j) for turn in turns for j in range(side)]
        targets = [at(j, lax.rem(turn + j, side)) for turn, j in places]
        blocks = blk_ref[...]
        placing = jnp.concatenate(
            [
                onehot(
                    iota((quarter, points), 0).astype(F32).astype(BF16),
                    jnp.where(blocks == target, high, -1.0).astype(BF16),
                )
                for target in targets
            ],
            axis=0,
        )
        packed = lax.dot_general(placing, expanded[...], NT, preferred_element_type=F32)
        packed = packed.astype(BF16)
        for k, target in enumerate(targets):
            turn, j = places[k]
            slot = turn * side + j
            mine = packed[k * quarter : (k + 1) * quarter]

            def fill(pack):
                pack[slot, 0:quarter, :] = mine[:, 0:128]
                pack[slot, quarter : 2 * quarter, :] = mine[:, 128:256]

            def ship():
                fill(send)
                copy_to(slot, target).start()

            if j == 0:

                pl.when(turn == 0)(lambda: fill(recv))
                pl.when(turn != 0)(ship)
            else:
                ship()
        return carry

    lax.fori_loop(0, side // 2, send_group, 0)

    loads[2].wait()
    build_weights(one_ref, wide_one)
    loads[3].wait()
    build_weights(two_ref, wide_two)

    sums[...] = jnp.zeros_like(sums)
    counts[...] = jnp.zeros_like(counts)

    pieces = cap // 128
    names = iota((ROWS, 128), 0).astype(F32).astype(BF16)

    def slot_at(turn):
        return jnp.where(turn == 0, 0, lax.rem(turn + side - 2, columns - 1) + 1)

    def arrive(copy, turn, first):
        if first:
            pl.when(turn != 0)(lambda: copy(slot_at(turn), block).wait_recv())
        else:
            copy(slot_at(turn), block).wait_recv()

    def count_group(step, carry):
        tables = ([], [])
        for j in range(BATCH):
            turn = step * BATCH + j
            arrive(code_copy, turn, j == 0)
            code = codes_in[slot_at(turn)].astype(F32)
            for table, value in zip(tables, (code[0:8] - 1.0, code[8:16])):
                for k in range(pieces):
                    table.append(onehot(names[:64], value[k : k + 1].astype(BF16)))
        coarse, fine = [jnp.concatenate(table, axis=1) for table in tables]
        counts[...] += lax.dot_general(coarse, fine, NT, preferred_element_type=F32)
        return carry

    lax.fori_loop(0, columns // BATCH, count_group, 0)
    tally = pltpu.einshape("a(bc)->(ab)c", counts[...], b=ZG)
    share = jnp.where(tally > 0.5, 1.0 / jnp.maximum(tally, 1.0), 0.0)
    first = share.astype(BF16)
    rest = share - first.astype(F32)
    second = rest.astype(BF16)
    third_part = (rest - second.astype(F32)).astype(BF16)
    spread = jnp.where(iota((BE, BE * C), 0) == iota((BE, BE * C), 1) // C, 1.0, 0.0).astype(BF16)
    inverse[...] = (
        jnp.dot(first, spread, preferred_element_type=F32)
        + jnp.dot(second, spread, preferred_element_type=F32)
        + jnp.dot(third_part, spread, preferred_element_type=F32)
    )


    def bin_group(base, size):
        hots, masked = [], []
        for j in range(size):
            turn = base + j
            slot = slot_at(turn)
            arrive(copy_to, turn, j == 0)
            code = codes_in[slot].astype(F32)
            a = code[0:8].astype(jnp.int32) - 1
            b = code[8:16].astype(jnp.int32)
            flat = a * 4 + (b >> 4)
            deep = (b >> 2) & 3
            inner = (b & 3).astype(F32)
            flat = flat.astype(F32)
            by_group = []
            for group in range(ZG):
                row = jnp.where(deep == group, flat, -1.0)
                by_group.append(
                    jnp.concatenate(
                        [onehot(names, row[k : k + 1].astype(BF16)) for k in range(pieces)], axis=1
                    )
                )
            hots.append(jnp.concatenate(by_group, axis=0))
            turned = inner.T
            of_lane = (iota((128, WIDE), 1) // C).astype(F32)
            choose = jnp.concatenate(
                [(turned[:, k : k + 1] == of_lane).astype(F32) for k in range(pieces)], axis=0
            ).astype(BF16)
            quads = []
            for k in range(4):
                start, col = k // 2 * quarter, k % 2 * C
                piece = recv[slot, start : start + quarter, col : col + C]
                quads.append(jnp.concatenate([piece] * 4, axis=1))
            masked.append(jnp.concatenate(quads, axis=0) * choose)
        hot = jnp.concatenate(hots, axis=1)
        sums[...] += jnp.dot(hot, jnp.concatenate(masked, axis=0), preferred_element_type=F32)

    lax.fori_loop(
        0, columns // BATCH, lambda step, carry: (bin_group(step * BATCH, BATCH), carry)[1], 0
    )

    keep_y = (link_ref[0, 2] >= 0).astype(F32)
    keep_z = (link_ref[0, 4] >= 0).astype(F32)

    def side_copy(layer, up):
        k = 2 * layer + up
        return pltpu.make_async_remote_copy(
            src_ref=(hidden if layer else voxels).at[pl.ds((ROWS - BE) * up, BE)],
            dst_ref=side_in.at[k],
            send_sem=side_send.at[k],
            recv_sem=side_recv.at[k],
            device_id=(region + 1 if up else region - 1, block),
            device_id_type=MESH,
        )

    def send_sides(layer):
        pl.when(region > 0)(lambda: side_copy(layer, 0).start())
        pl.when(region < regions - 1)(lambda: side_copy(layer, 1).start())

    def receive_sides(layer):
        def put(k, plane):
            groups = [side_in[k, :, z * WIDE : (z + 1) * WIDE].astype(F32) for z in range(ZG)]
            place_plane(field.at[layer], plane, groups, 0.0, 0.0)

        def blank(plane):
            field[layer, :, plane * BE : (plane + 1) * BE, :] = jnp.zeros((3, BE, ZPAD), BF16)

        @pl.when(region > 0)
        def _():
            side_copy(layer, 1).wait_recv()
            put(2 * layer + 1, 0)

        @pl.when(region < regions - 1)
        def _():
            side_copy(layer, 0).wait_recv()
            put(2 * layer, BE + 1)

        pl.when(region == 0)(lambda: blank(0))
        pl.when(region == regions - 1)(lambda: blank(BE + 1))

    def settle_sides(layer):
        pl.when(region > 0)(lambda: side_copy(layer, 0).wait_send())
        pl.when(region < regions - 1)(lambda: side_copy(layer, 1).wait_send())

    def mean_plane(x):
        rows = slice(x * BE, (x + 1) * BE)
        for z in range(ZG):
            total = sums[z * ROWS + x * BE : z * ROWS + (x + 1) * BE, :]
            mean = (total * inverse[rows, z * WIDE : (z + 1) * WIDE]).astype(BF16)
            voxels[rows, z * WIDE : (z + 1) * WIDE] = mean

    def place_mean(x):
        groups = [
            voxels[x * BE : (x + 1) * BE, z * WIDE : (z + 1) * WIDE].astype(F32) for z in range(ZG)
        ]
        place_plane(field.at[0], x + 1, groups, keep_y, keep_z)

    mean_plane(0)
    mean_plane(BE - 1)
    send_sides(0)
    for x in range(1, BE - 1):
        mean_plane(x)
    for x in range(BE):
        place_mean(x)

    def encode(layer, runs, bias, target):
        total = convolve(field.at[layer], wide_two if layer else wide_one, runs)
        start = 0
        for group in range(ZG):
            cols = slice(group * WIDE, (group + 1) * WIDE)
            for p, n in runs:
                rows = slice(p * BE, (p + n) * BE)
                value = total[start : start + n * BE] + bias
                start += n * BE
                if layer:
                    value = value + voxels[rows, cols].astype(F32)
                value = jnp.where(inverse[rows, cols] > 0.0, jnp.maximum(value, 0.0), 0.0)
                target[rows, cols] = value.astype(BF16)

    def place_hidden(x):
        rows = pl.ds(pl.multiple_of(x * BE, BE), BE)
        groups = [hidden[rows, z * WIDE : (z + 1) * WIDE].astype(F32) for z in range(ZG)]
        place_plane(field.at[1], x + 1, groups, keep_y, keep_z)

    bias_one = jnp.concatenate([bone_ref[...]] * 4, axis=1)
    bias_two = jnp.concatenate([btwo_ref[...]] * 4, axis=1)

    middle, ends = [(1, BE - 2)], [(0, 1), (BE - 1, 1)]
    encode(0, middle, bias_one, hidden)
    receive_sides(0)
    encode(0, ends, bias_one, hidden)
    send_sides(1)
    lax.fori_loop(0, BE, lambda x, carry: (place_hidden(x), carry)[1], 0, unroll=UNROLL)
    spans = [slice(BE, ROWS - BE), slice(0, BE), slice(ROWS - BE, ROWS)]
    saves = [
        pltpu.make_async_copy(result.at[rows], out_hbm.at[rows], save_sem.at[k])
        for k, rows in enumerate(spans)
    ]
    encode(1, middle, bias_two, result)
    saves[0].start()
    receive_sides(1)
    encode(1, ends, bias_two, result)
    saves[1].start()
    saves[2].start()

    def settle(slot, carry):
        copy_to(slot, block).wait_send()
        code_copy(slot, block).wait_send()
        return carry

    lax.fori_loop(1, columns, settle, 0)
    settle_sides(0)
    settle_sides(1)
    for save in saves:
        save.wait()


def unfold(flat_ref, out_hbm, tiles, sems):
    copies = []
    step = ROWS // PARTS
    for k in range(PARTS):
        rows = slice(k * step, (k + 1) * step)
        tiles[rows] = pltpu.einshape("a(bc)->abc", flat_ref[rows, :], b=BE)
        copies.append(pltpu.make_async_copy(tiles.at[rows], out_hbm.at[rows], sems.at[k]))
        copies[-1].start()
    for copy in copies:
        copy.wait()


def per_device(
    dims, point_feats, point_block, point_voxel, neighbours, conv_one, bias_one, conv_two, bias_two
):
    regions, columns = dims
    points = point_feats.shape[0]
    quarter = 2 * points // columns // 4
    vmem = pl.BlockSpec(memory_space=pltpu.VMEM)
    smem = pl.BlockSpec(memory_space=pltpu.SMEM)
    hbm = pl.BlockSpec(memory_space=pl.ANY)
    pack = pltpu.VMEM((columns, 2 * quarter, 128), BF16)
    flat = pl.pallas_call(
        functools.partial(body, dims),
        out_shape=jax.ShapeDtypeStruct((ROWS, BE * C), BF16),
        in_specs=[hbm, vmem, hbm, smem, hbm, vmem, hbm, vmem],
        out_specs=hbm,
        scratch_shapes=[
            pltpu.VMEM((C, points), BF16),
            pltpu.VMEM((1, points), jnp.int32),
            pltpu.VMEM((27, C, C), BF16),
            pltpu.VMEM((27, C, C), BF16),
            pltpu.VMEM((WIDE, points), BF16),
            pltpu.VMEM((columns * 16, 128), BF16),
            pltpu.VMEM((columns, 16, 128), BF16),
            pack,
            pack,
            pltpu.VMEM((ZG * ROWS, WIDE), F32),
            pltpu.VMEM((64, 64), F32),
            pltpu.VMEM((ROWS, BE * C), F32),
            pltpu.VMEM((ROWS, BE * C), BF16),
            pltpu.VMEM((ROWS, BE * C), BF16),
            pltpu.VMEM((2, 3, (BE + 2) * BE, ZPAD), BF16),
            pltpu.VMEM((9 * TAP, WIDE), BF16),
            pltpu.VMEM((9 * TAP, WIDE), BF16),
            pltpu.VMEM((4, BE, BE * C), BF16),
            pltpu.SemaphoreType.DMA((columns,)),
            pltpu.SemaphoreType.DMA((columns,)),
            pltpu.SemaphoreType.DMA((4,)),
            pltpu.SemaphoreType.DMA((4,)),
            pltpu.SemaphoreType.DMA((4,)),
            pltpu.SemaphoreType.DMA((columns,)),
            pltpu.SemaphoreType.DMA((columns,)),
            pltpu.VMEM((ROWS, BE * C), BF16),
            pltpu.SemaphoreType.DMA((3,)),
        ],
        compiler_params=pltpu.CompilerParams(
            collective_id=0, has_side_effects=True, vmem_limit_bytes=60 * 2**20
        ),
    )(
        point_feats.T,
        point_block.T,
        point_voxel.reshape(1, points),
        neighbours,
        conv_one,
        bias_one.reshape(1, C),
        conv_two,
        bias_two.reshape(1, C),
    )
    out = pl.pallas_call(
        unfold,
        out_shape=jax.ShapeDtypeStruct((ROWS, BE, C), BF16),
        in_specs=[vmem],
        out_specs=hbm,
        scratch_shapes=[pltpu.VMEM((ROWS, BE, C), BF16), pltpu.SemaphoreType.DMA((PARTS,))],
        compiler_params=pltpu.CompilerParams(vmem_limit_bytes=8 * 2**20),
    )(flat)
    return out.reshape(1, BE, BE, BE, C)


def solution(mesh):
    dims = (mesh.shape["region"], mesh.shape["block"])
    return jax.shard_map(
        functools.partial(per_device, dims),
        mesh=mesh,
        in_specs=(
            P(("region", "block"), None),
            P(("region", "block"), None),
            P(("region", "block")),
            P(("region", "block"), None),
            P(),
            P(),
            P(),
            P(),
        ),
        out_specs=P(("region", "block"), None, None, None, None),
        check_vma=False,
    )
```
